32 devices in a mesh: ctx: 8 (over z, x), tp: 4 (over y, core).
Axes of the slice: x: 2, y: 2, z: 4, core: 2. Of those that a mesh axis runs over, the one named last changes fastest.
Arguments:
- queries: bfloat16 [2048, 2048], P('ctx', 'tp'), may hold values from -6 to 6
- keys: bfloat16 [2048, 512], P('ctx', 'tp'), may hold values from -6 to 6
- values: bfloat16 [2048, 512], P('ctx', 'tp'), may hold values from -6 to 6
- outputs: bfloat16 [2048, 2048], P('ctx', 'tp'), may hold values from -6 to 6
- out_grad: bfloat16 [2048, 2048], P('ctx', 'tp'), may hold values from -6 to 6
- log_norm: float32 [2048, 16], P('ctx', 'tp'), as said below
- block_mask: int32 [8, 4], P('ctx'), may hold values from 0 to 1, as said below
- counter_base: int32 [2], replicated, may hold values from 0 to 1048575
- q_weight: bfloat16 [4096, 2048], P(None, 'tp'), may hold values from -0.125 to 0.125
- k_weight: bfloat16 [4096, 512], P(None, 'tp'), may hold values from -0.09375 to 0.09375
- v_weight: bfloat16 [4096, 512], P(None, 'tp'), may hold values from -0.09375 to 0.09375
Outputs:
- input_grad: bfloat16 [2048, 4096], P('ctx', 'tp')
The draws below stay inside these ranges and needn't reach their ends.
Inputs may be any that keep to these rules, and one draw needn't show every extreme that they name: block_mask[i, r] is 1 where query block i attends to key block i - r; column 0 and the row of the last block are all 1. log_norm lies between log(512) - 0.5 and log(512) + 2.5.
All inputs are finite; a program needn't handle non-finite values.
Results may differ from the reference program's by a relative error of at most 0.015.
Values may be sent and summed in bfloat16 or wider, within the bound.
No kernel may reach another device: no remote copies, remote signals or barrier semaphores. Data moves between devices by JAX's collectives and lax.ppermute only.
A program may use at most 64 MiB of HBM per device.

```python
import math
import jax
import jax.numpy as jnp
from jax import lax

TOK = 256
D = 4096
HD = 128
HQ_DEV = 4
STEPS = 4
NBLK = 8
SEQ = 2048
HEADS = 16
WIN = 896
N_TP = 4


def draw_log_norm(key, part):
    centre = math.log(2.0 * TOK)
    spread = jax.random.uniform(key, (SEQ, HEADS), jnp.float32, 0.0, 1.5)
    return (centre + spread).astype(jnp.float32)


def draw_block_mask(key, part):
    random_bits = jax.random.randint(key, (NBLK, STEPS), 0, 2, dtype=jnp.int32)
    first_col = jnp.arange(STEPS, dtype=jnp.int32)[None, :] == 0
    last_row = jnp.arange(NBLK, dtype=jnp.int32)[:, None] == NBLK - 1
    return jnp.where(first_col | last_row, jnp.int32(1), random_bits).astype(jnp.int32)


def raised(result, key, source, target, parts, factor):
    owner, partner = [(jnp.arange(result.shape[position]) // (result.shape[position] // parts)).reshape([-1 if axis == position else 1 for axis in range(result.ndim)]) for position in (source, target)]
    chosen = jax.random.permutation(key, parts)[partner]
    strong = (owner == chosen) | (owner == (partner + parts // 2) % parts)
    return jnp.where(strong, factor * result, result)


def shard_levels(rng, dims, cuts, smallest, top_value):
    factor_of = 1.0
    for axis_at, blocks in cuts:
        draws = jax.random.uniform(jax.random.fold_in(jax.random.fold_in(rng, 6), axis_at), (blocks,), jnp.float32, smallest / len(cuts), top_value / len(cuts))
        factor_of = factor_of * jnp.repeat(jnp.exp(draws), dims[axis_at] // blocks).reshape((-1,) + (1,) * (len(dims) - 1 - axis_at))
    return factor_of


def bell_draw(own_key, extent, deviation, reach, cuts=(), held_as=jnp.bfloat16):
    values = jax.random.normal(own_key, extent, jnp.float32) * deviation
    if len(cuts) > 0:
        values = shard_levels(own_key, extent, cuts, -0.22, 0.18) * values
    return jnp.clip(values, min=-reach, max=reach).astype(held_as)


def heavy_noise(stream_key, extent, scale, most, cuts, heavy, kind=jnp.bfloat16):
    result = scale * jax.random.normal(stream_key, extent, jnp.float32)
    if cuts:
        result = result * shard_levels(stream_key, extent, cuts, -0.22, 0.18)
    return jnp.clip(raised(result, jax.random.fold_in(stream_key, 3), *heavy), -most, most).astype(kind)


def setup_inputs(seed: int = 0) -> dict:
    splits = jax.random.split(jax.random.key(seed), 12)
    queries = bell_draw(splits[0], (SEQ, HEADS * HD), 1.0, 6.0, ((0, 8), (1, 4)))
    keys = bell_draw(splits[1], (SEQ, N_TP * HD), 1.0, 6.0, ((0, 8), (1, 4)))
    values = bell_draw(splits[2], (SEQ, N_TP * HD), 1.0, 6.0, ((0, 8), (1, 4)))
    outputs = bell_draw(splits[3], (SEQ, HEADS * HD), 1.0, 6.0, ((0, 8), (1, 4)))
    out_grad = bell_draw(splits[4], (SEQ, HEADS * HD), 1.0, 6.0, ((0, 8), (1, 4)))
    log_norm = draw_log_norm(jax.random.fold_in(splits[11], 71), 0)
    block_mask = draw_block_mask(jax.random.fold_in(splits[11], 71), 0)
    counter_base = jax.random.randint(splits[7], (2,), 0, 1048576).astype(jnp.int32)
    q_weight = heavy_noise(splits[8], (D, HEADS * HD), D ** -0.5, 0.125, ((1, 4),), (1, 0, 4, 2.0))
    k_weight = bell_draw(splits[9], (D, N_TP * HD), D ** -0.5, 0.09375, ((1, 4),))
    v_weight = bell_draw(splits[10], (D, N_TP * HD), D ** -0.5, 0.09375, ((1, 4),))
    return {"queries": queries, "keys": keys, "values": values, "outputs": outputs, "out_grad": out_grad, "log_norm": log_norm, "block_mask": block_mask, "counter_base": counter_base, "q_weight": q_weight, "k_weight": k_weight, "v_weight": v_weight}


keep_level = 103
keep_scale = 1024.0 / 921.0


def keep_mask(head_ids, query_pos, key_pos, seed_value):
    mixed = head_ids[:, None, None] * 83492791 + query_pos[None, :, None] * 73856093 + key_pos[None, None, :] * 19349663 + seed_value
    mixed = mixed ^ lax.shift_right_logical(mixed, jnp.int32(15))
    mixed = mixed * 739982445
    mixed = mixed ^ lax.shift_right_logical(mixed, jnp.int32(12))
    mixed = mixed * 695872825
    mixed = mixed ^ lax.shift_right_logical(mixed, jnp.int32(15))
    return (mixed & 1023) >= keep_level


def pair_grads(query_blk, grad_out, norm_blk, row_delta, key_blk, value_blk, query_start, key_start, active, head_ids, counter_base, window):
    rows_count = query_blk.shape[0]
    scaling = query_blk.shape[2] ** -0.5
    scores = jnp.einsum("qhd,kd->hqk", query_blk.astype(jnp.float32), key_blk.astype(jnp.float32)) * scaling
    query_pos = query_start + jnp.arange(rows_count, dtype=jnp.int32)
    key_pos = key_start + jnp.arange(rows_count, dtype=jnp.int32)
    spacing = query_pos[:, None] - key_pos[None, :]
    allowed = (spacing >= 0) & (spacing < window) & active
    probs = jnp.where(allowed[None], jnp.exp(scores - jnp.transpose(norm_blk)[:, :, None]), jnp.float32(0.0))
    kept = keep_mask(head_ids, query_pos + counter_base[1], key_pos + counter_base[1], counter_base[0])
    dropped = jnp.where(kept, probs * keep_scale, jnp.float32(0.0)).astype(jnp.bfloat16)
    grad_value = jnp.einsum("hqk,qhd->kd", dropped.astype(jnp.float32), grad_out.astype(jnp.float32))
    grad_probs = jnp.einsum("qhd,kd->hqk", grad_out.astype(jnp.float32), value_blk.astype(jnp.float32))
    grad_scores = (probs * (jnp.where(kept, grad_probs * keep_scale, jnp.float32(0.0)) - jnp.transpose(row_delta)[:, :, None])).astype(jnp.bfloat16)
    grad_query = jnp.einsum("hqk,kd->qhd", grad_scores.astype(jnp.float32), key_blk.astype(jnp.float32)) * scaling
    grad_key = jnp.einsum("hqk,qhd->kd", grad_scores.astype(jnp.float32), query_blk.astype(jnp.float32)) * scaling
    return grad_query, grad_key, grad_value


def by_group(array, inner_cols):
    return jnp.transpose(array.reshape(array.shape[0], N_TP, inner_cols), (1, 0, 2))


def reference(queries, keys, values, outputs, out_grad, log_norm, block_mask, counter_base, q_weight, k_weight, v_weight):
    seq_len = NBLK * TOK
    head_width = HQ_DEV * HD
    grouped = (by_group(queries, head_width), by_group(keys, HD), by_group(values, HD), by_group(outputs, head_width), by_group(out_grad, head_width), by_group(log_norm, HQ_DEV), by_group(q_weight, head_width), by_group(k_weight, HD), by_group(v_weight, HD), jnp.arange(N_TP, dtype=jnp.int32))

    def group_step(summed, pieces):
        query_g, key_g, value_g, output_g, grad_g, norm_g, weight_q, weight_k, weight_v, group_id = pieces
        query_blocks = query_g.reshape(NBLK, TOK, HQ_DEV, HD)
        grad_blocks = grad_g.reshape(NBLK, TOK, HQ_DEV, HD)
        delta_all = jnp.sum(grad_g.astype(jnp.float32).reshape(seq_len, HQ_DEV, HD) * output_g.astype(jnp.float32).reshape(seq_len, HQ_DEV, HD), axis=2)
        delta_blocks = delta_all.reshape(NBLK, TOK, HQ_DEV)
        norm_blocks = norm_g.reshape(NBLK, TOK, HQ_DEV)
        key_blocks = key_g.reshape(NBLK, TOK, HD)
        value_blocks = value_g.reshape(NBLK, TOK, HD)
        head_ids = group_id * HQ_DEV + jnp.arange(HQ_DEV, dtype=jnp.int32)

        def per_block(block_id):
            grad_query = jnp.zeros((TOK, HQ_DEV, HD), jnp.float32)
            key_terms = []
            value_terms = []
            for offset in range(STEPS):
                source = jnp.maximum(block_id - offset, 0).astype(jnp.int32)
                active = (block_id - offset >= 0) & (block_mask[block_id, offset] == 1)
                add_query, add_key, add_value = pair_grads(query_blocks[block_id], grad_blocks[block_id], norm_blocks[block_id], delta_blocks[block_id], key_blocks[source], value_blocks[source], block_id * TOK, source * TOK, active, head_ids, counter_base, WIN)
                grad_query = grad_query + add_query
                key_terms.append(add_key)
                value_terms.append(add_value)
            return grad_query, jnp.stack(key_terms), jnp.stack(value_terms)

        grad_query, key_contrib, value_contrib = lax.map(per_block, jnp.arange(NBLK, dtype=jnp.int32))
        grad_key = jnp.zeros((NBLK, TOK, HD), jnp.float32)
        grad_value = jnp.zeros((NBLK, TOK, HD), jnp.float32)
        for offset in range(STEPS):
            padding = jnp.zeros((offset, TOK, HD), jnp.float32)
            grad_key = grad_key + jnp.concatenate([key_contrib[offset:, offset], padding], axis=0)
            grad_value = grad_value + jnp.concatenate([value_contrib[offset:, offset], padding], axis=0)
        query_round = grad_query.reshape(seq_len, head_width).astype(jnp.bfloat16)
        key_round = grad_key.reshape(seq_len, HD).astype(jnp.bfloat16)
        value_round = grad_value.reshape(seq_len, HD).astype(jnp.bfloat16)
        partial_term = jnp.dot(query_round, weight_q.T, preferred_element_type=jnp.float32)
        partial_term = partial_term + jnp.dot(key_round, weight_k.T, preferred_element_type=jnp.float32)
        partial_term = partial_term + jnp.dot(value_round, weight_v.T, preferred_element_type=jnp.float32)
        rounded = lax.optimization_barrier(partial_term.astype(jnp.bfloat16))
        return summed + rounded.astype(jnp.float32), None

    summed, unused = lax.scan(group_step, jnp.zeros((seq_len, D), jnp.float32), grouped)
    return summed.astype(jnp.bfloat16)
```

```python
import functools
import math

import jax
import jax.numpy as jnp
from jax import lax
from jax.experimental import pallas as pl
from jax.experimental.pallas import tpu as pltpu
from jax.sharding import PartitionSpec as P

keep_level = 103
keep_scale = 1024.0 / 921.0
log2_e = math.log2(math.e)
f32, bf16, i32 = jnp.float32, jnp.bfloat16, jnp.int32
in_vmem = pl.BlockSpec(memory_space=pltpu.VMEM)
in_smem = pl.BlockSpec(memory_space=pltpu.SMEM)
chunks = 2


def cyclic(array, axis, by):
    count = lax.axis_size(axis)
    return lax.ppermute(array, axis, [(i, (i + by) % count) for i in range(count)])


def other_core(array):
    count = lax.axis_size("tp")
    return lax.ppermute(array, "tp", [(i, i ^ 1) for i in range(count)])


def dot(left, right, left_dim, right_dim):
    return lax.dot_general(
        left, right, (((left_dim,), (right_dim,)), ((), ())), preferred_element_type=f32
    )


def keep_mask(mixed):
    mixed = mixed ^ lax.shift_right_logical(mixed, i32(15))
    mixed = mixed * i32(739982445)
    mixed = mixed ^ lax.shift_right_logical(mixed, i32(12))
    mixed = mixed * i32(695872825)
    mixed = mixed ^ lax.shift_right_logical(mixed, i32(15))
    return (mixed & i32(1023)) >= i32(keep_level)


def block_grads(offset, window, heads, counter_ref, key, value, query_ref, grad_ref, rows_ref):
    rows, width = key.shape
    block_id = lax.axis_index("ctx")
    first_head = lax.axis_index("tp") * heads
    seed, base = counter_ref[0], counter_ref[1]
    key_index = lax.broadcasted_iota(i32, (rows, rows), 0)
    query_index = lax.broadcasted_iota(i32, (rows, rows), 1)
    key_part = (key_index + (base + (block_id - offset) * rows)) * i32(19349663)
    query_part = (
        lax.broadcasted_iota(i32, (1, rows), 1) + (base + block_id * rows)
    ) * i32(73856093) + seed
    key_t = key.T
    scale = log2_e * width**-0.5
    key_sum = value_sum = None
    query_parts = []
    for head in range(heads):
        cols = pl.ds(head * width, width)
        query, grad = query_ref[:, cols], grad_ref[:, cols]
        log_norm = rows_ref[pl.ds(head, 1), :]
        row_delta = rows_ref[pl.ds(heads + head, 1), :]
        kept = keep_mask(key_part + (query_part + (first_head + head) * i32(83492791)))
        probs = jnp.exp2(dot(key, query, 1, 1) * scale - log_norm)
        spacing = query_index - key_index
        if offset == 0:
            probs = jnp.where(spacing >= 0, probs, f32(0.0))
        if (offset + 1) * rows > window:
            probs = jnp.where(spacing < window - offset * rows, probs, f32(0.0))
        dropped = jnp.where(kept, probs, f32(0.0)).astype(bf16)
        grad_probs = dot(value, grad, 1, 1)
        grad_scores = (
            probs * (jnp.where(kept, grad_probs, f32(0.0)) - row_delta)
        ).astype(bf16)
        value_add = dot(dropped, grad, 1, 0)
        key_add = dot(grad_scores, query, 1, 0)
        key_sum = key_add if head == 0 else key_sum + key_add
        value_sum = value_add if head == 0 else value_sum + value_add
        query_parts.append(dot(key_t, grad_scores, 1, 0))
    return key_sum, value_sum, query_parts


def own_kernel(
    window, heads, counter_ref, key_ref, value_ref, query_ref, grad_ref, output_ref, norm_ref,
    rows_ref, total_ref, sums_ref,
):
    rows, width = key_ref.shape
    lane = lax.broadcasted_iota(i32, (rows, 128), 1)
    packed = jnp.zeros((rows, 128), f32)
    for head in range(heads):
        cols = pl.ds(head * width, width)
        delta = jnp.sum(
            grad_ref[:, cols].astype(f32) * output_ref[:, cols].astype(f32), axis=1, keepdims=True
        )
        packed = jnp.where(lane == heads + head, delta * f32(1.0 / keep_scale), packed)
        packed = jnp.where(lane == head, norm_ref[:, head : head + 1] * f32(log2_e), packed)
    rows_ref[...] = packed.T[: 2 * heads]
    key_sum, value_sum, query_parts = block_grads(
        0, window, heads, counter_ref, key_ref[...], value_ref[...], query_ref, grad_ref, rows_ref
    )
    grad_scale = keep_scale * width**-0.5
    sums_ref[:, :width] = key_sum * f32(grad_scale)
    sums_ref[:, width:] = value_sum * f32(keep_scale)
    for head, part in enumerate(query_parts):
        total_ref[:, pl.ds(head * rows, rows)] = part


def pair_kernel(
    offset, window, heads, last, counter_ref, mask_ref, key_value_ref, query_ref, grad_ref,
    rows_ref, before_ref, total_ref, sums_ref,
):
    rows = key_value_ref.shape[0]
    width = key_value_ref.shape[1] // 2
    active = (lax.axis_index("ctx") >= offset) & (mask_ref[0, offset] == 1)
    grad_scale = keep_scale * width**-0.5

    @pl.when(active)
    def _():
        key_sum, value_sum, query_parts = block_grads(
            offset, window, heads, counter_ref, key_value_ref[:, :width], key_value_ref[:, width:],
            query_ref, grad_ref, rows_ref,
        )
        sums_ref[:, :width] = (key_sum * f32(grad_scale)).astype(bf16)
        sums_ref[:, width:] = (value_sum * f32(keep_scale)).astype(bf16)
        for head, part in enumerate(query_parts):
            cols = pl.ds(head * rows, rows)
            if last:
                total_ref[:, pl.ds(head * width, width)] = (
                    (before_ref[:, cols] + part).T * f32(grad_scale)
                ).astype(bf16)
            else:
                total_ref[:, cols] = before_ref[:, cols] + part

    @pl.when(jnp.logical_not(active))
    def _():
        sums_ref[...] = jnp.zeros(sums_ref.shape, bf16)
        for head in range(heads):
            cols = pl.ds(head * rows, rows)
            if last:
                total_ref[:, pl.ds(head * width, width)] = (
                    before_ref[:, cols].T * f32(grad_scale)
                ).astype(bf16)
            else:
                total_ref[:, cols] = before_ref[:, cols]


def project_kernel(at_ref, *refs):
    count = (len(refs) - 1) // 2
    total = None
    for left, right in zip(refs[:count], refs[count:-1]):
        part = dot(left[...], right[...], 1, 1)
        total = part if total is None else total + part
    refs[-1][...] = total.astype(bf16)


def project(at, step, cols, lefts, rights):
    rows = lefts[0].shape[0]
    return pl.pallas_call(
        project_kernel,
        grid_spec=pltpu.PrefetchScalarGridSpec(
            num_scalar_prefetch=1,
            grid=(cols // step,),
            in_specs=[pl.BlockSpec(left.shape, lambda i, at: (0, 0)) for left in lefts]
            + [pl.BlockSpec((step, right.shape[1]), lambda i, at: (at[0] + i, 0)) for right in rights],
            out_specs=pl.BlockSpec((rows, step), lambda i, at: (0, i)),
        ),
        out_shape=jax.ShapeDtypeStruct((rows, cols), bf16),
        compiler_params=pltpu.CompilerParams(vmem_limit_bytes=32 * 2**20),
        name="project",
    )(at, *lefts, *rights)


def on_device(
    queries,
    keys,
    values,
    outputs,
    out_grad,
    log_norm,
    block_mask,
    counter_base,
    q_weight,
    k_weight,
    v_weight,
):
    rows, width = keys.shape
    heads = log_norm.shape[1]
    steps = block_mask.shape[1]
    window = 3 * rows + rows // 2
    tp_size = lax.axis_size("tp")
    tp_id = lax.axis_index("tp")
    params = pltpu.CompilerParams(vmem_limit_bytes=48 * 2**20)

    key_value = jnp.concatenate([keys, values], axis=1)
    arrived = {offset: cyclic(key_value, "ctx", offset) for offset in range(1, steps)}
    weights = (q_weight, k_weight, v_weight)
    other_weights = tuple(other_core(weight) for weight in weights)

    row_values, total, own_sums = pl.pallas_call(
        functools.partial(own_kernel, window, heads),
        in_specs=[in_smem] + [in_vmem] * 6,
        out_specs=[in_vmem] * 3,
        out_shape=[
            jax.ShapeDtypeStruct((2 * heads, rows), f32),
            jax.ShapeDtypeStruct((width, heads * rows), f32),
            jax.ShapeDtypeStruct((rows, 2 * width), f32),
        ],
        compiler_params=params,
        name="own_block",
    )(counter_base, keys, values, queries, out_grad, outputs, log_norm)

    returned = []
    for offset in range(1, steps):
        last = offset == steps - 1
        total, sums = pl.pallas_call(
            functools.partial(pair_kernel, offset, window, heads, last),
            in_specs=[in_smem] * 2 + [in_vmem] * 5,
            out_specs=[in_vmem] * 2,
            out_shape=[
                jax.ShapeDtypeStruct((rows, heads * width), bf16)
                if last
                else jax.ShapeDtypeStruct((width, heads * rows), f32),
                jax.ShapeDtypeStruct((rows, 2 * width), bf16),
            ],
            compiler_params=params,
            name="block_back_%d" % offset,
        )(counter_base, block_mask, arrived[offset], queries, out_grad, row_values, total)
        returned.append(cyclic(sums, "ctx", -offset))
    grad_query = total
    other_query = other_core(grad_query)
    sums = own_sums
    for item in returned:
        sums = sums + item.astype(f32)
    sums = sums.astype(bf16)
    other_sums = other_core(sums)

    lefts = [grad_query, other_query, sums, other_sums]
    key_value_w = [
        jnp.concatenate([pair[0], pair[1]], axis=1)
        for pair in ((k_weight, v_weight), other_weights[1:])
    ]
    rights = [q_weight, other_weights[0], *key_value_w]
    cols = q_weight.shape[0] // tp_size
    piece = cols // chunks
    step = min(piece, 256)
    mine = None
    sent = []
    for hop in range(2, tp_size, 2):
        target = lax.rem(tp_id + hop, tp_size)
        parts = []
        for chunk in range(chunks):
            at = (target * (cols // step) + chunk * (piece // step)).astype(i32).reshape(1)
            part = project(at, step, piece, lefts, rights)
            parts.append(cyclic(part, "tp", hop))
        sent.append(parts)
    at = (tp_id * (cols // step)).astype(i32).reshape(1)
    mine = project(at, step, cols, lefts, rights).astype(f32)
    for parts in sent:
        mine = mine + jnp.concatenate(parts, axis=1).astype(f32)
    return mine.astype(bf16)


def solution(mesh):
    return jax.shard_map(
        on_device,
        mesh=mesh,
        in_specs=(
            P("ctx", "tp"),
            P("ctx", "tp"),
            P("ctx", "tp"),
            P("ctx", "tp"),
            P("ctx", "tp"),
            P("ctx", "tp"),
            P("ctx", None),
            P(),
            P(None, "tp"),
            P(None, "tp"),
            P(None, "tp"),
        ),
        out_specs=P("ctx", "tp"),
        check_vma=False,
    )
```

```python
import functools
import math

import jax
import jax.numpy as jnp
from jax import lax
from jax.experimental import pallas as pl
from jax.experimental.pallas import tpu as pltpu
from jax.sharding import PartitionSpec as P

keep_level = 103
keep_scale = 1024.0 / 921.0
log2_e = math.log2(math.e)
f32, bf16, i32 = jnp.float32, jnp.bfloat16, jnp.int32
in_vmem = pl.BlockSpec(memory_space=pltpu.VMEM)
in_hbm = pl.BlockSpec(memory_space=pltpu.HBM)
in_smem = pl.BlockSpec(memory_space=pltpu.SMEM)


def from_hbm(array):
    return pltpu.with_memory_space_constraint(array, pltpu.HBM)


def cyclic(array, axis, by):
    count = lax.axis_size(axis)
    return lax.ppermute(array, axis, [(i, (i + by) % count) for i in range(count)])


def other_core(array):
    count = lax.axis_size("tp")
    return lax.ppermute(array, "tp", [(i, i ^ 1) for i in range(count)])


def dot(left, right, left_dim, right_dim):
    return lax.dot_general(
        left, right, (((left_dim,), (right_dim,)), ((), ())), preferred_element_type=f32
    )


def keep_mask(mixed):
    mixed = mixed ^ lax.shift_right_logical(mixed, i32(15))
    mixed = mixed * i32(739982445)
    mixed = mixed ^ lax.shift_right_logical(mixed, i32(12))
    mixed = mixed * i32(695872825)
    mixed = mixed ^ lax.shift_right_logical(mixed, i32(15))
    return (mixed & i32(1023)) >= i32(keep_level)


def block_grads(offset, window, heads, key, value, query_ref, grad_ref, mix_ref, norm_ref, delta_ref):
    rows, width = key.shape
    key_index = lax.broadcasted_iota(i32, (rows, rows), 0)
    query_index = lax.broadcasted_iota(i32, (rows, rows), 1)
    key_part = (key_index - offset * rows) * i32(19349663)
    key_t = key.T
    scale = log2_e * width**-0.5
    key_sum = value_sum = None
    query_parts = []
    for head in range(heads):
        cols = pl.ds(head * width, width)
        query, grad = query_ref[:, cols], grad_ref[:, cols]
        log_norm = norm_ref[pl.ds(offset * heads + head, 1), :]
        row_delta = delta_ref[pl.ds(head, 1), :]
        kept = keep_mask(key_part + mix_ref[pl.ds(head, 1), :])
        probs = jnp.exp2(dot(key, query, 1, 1) * scale - log_norm)
        spacing = query_index - key_index
        if offset == 0:
            probs = jnp.where(spacing >= 0, probs, f32(0.0))
        if (offset + 1) * rows > window:
            probs = jnp.where(spacing < window - offset * rows, probs, f32(0.0))
        dropped = jnp.where(kept, probs, f32(0.0)).astype(bf16)
        grad_probs = dot(value, grad, 1, 1)
        grad_scores = (
            probs * (jnp.where(kept, grad_probs, f32(0.0)) - row_delta)
        ).astype(bf16)
        value_add = dot(dropped, grad, 1, 0)
        key_add = dot(grad_scores, query, 1, 0)
        key_sum = key_add if head == 0 else key_sum + key_add
        value_sum = value_add if head == 0 else value_sum + value_add
        query_parts.append(dot(key_t, grad_scores, 1, 0))
    return key_sum, value_sum, query_parts


def load_kernel(
    heads, key_hbm, value_hbm, query_hbm, grad_hbm, output_hbm, norm_hbm, counter_hbm, mask_hbm,
    key_value, query, grad, output, mix_ref, rows_ref, norm_ref, counter_ref, mask_ref, sems,
):
    rows = key_hbm.shape[0]
    copies = [
        pltpu.make_async_copy(source, target, sems.at[i])
        for i, (source, target) in enumerate(
            (
                (key_hbm, key_value.at[pl.ds(0, rows)]),
                (value_hbm, key_value.at[pl.ds(rows, rows)]),
                (counter_hbm, counter_ref),
                (mask_hbm, mask_ref),
                (norm_hbm, norm_ref),
                (query_hbm, query),
                (grad_hbm, grad),
                (output_hbm, output),
            )
        )
    ]
    for copy in copies:
        copy.start()
    for copy in copies:
        copy.wait()
    block_id = lax.axis_index("ctx")
    first_head = lax.axis_index("tp") * heads
    base = counter_ref[1] + block_id * rows
    common = base * i32(19349663) + counter_ref[0]
    query_pos = lax.broadcasted_iota(i32, (1, rows), 1) + base
    for head in range(heads):
        mix_ref[pl.ds(head, 1), :] = query_pos * i32(73856093) + (
            common + (first_head + head) * i32(83492791)
        )
    norms = norm_ref[...] * f32(log2_e)
    for offset in range(mask_ref.shape[1]):
        active = (block_id >= offset) & (mask_ref[0, offset] == 1)
        rows_ref[pl.ds(offset * heads, heads), :] = jnp.where(active, norms, f32(jnp.inf))


def own_kernel(
    window, heads, key_value_ref, query_ref, grad_ref, output_ref, mix_ref, norm_ref, delta_ref,
    total_ref, sums_ref,
):
    rows, width = key_value_ref.shape[0] // 2, key_value_ref.shape[1]
    lane = lax.broadcasted_iota(i32, (rows, 128), 1)
    packed = jnp.zeros((rows, 128), f32)
    for head in range(heads):
        cols = pl.ds(head * width, width)
        delta = jnp.sum(
            grad_ref[:, cols].astype(f32) * output_ref[:, cols].astype(f32), axis=1, keepdims=True
        )
        packed = jnp.where(lane == head, delta * f32(1.0 / keep_scale), packed)
    delta_ref[...] = packed.T[: delta_ref.shape[0]]
    key_sum, value_sum, query_parts = block_grads(
        0, window, heads, key_value_ref[:rows], key_value_ref[rows:], query_ref, grad_ref, mix_ref,
        norm_ref, delta_ref,
    )
    grad_scale = keep_scale * width**-0.5
    sums_ref[:rows] = key_sum * f32(grad_scale)
    sums_ref[rows:] = value_sum * f32(keep_scale)
    for head, part in enumerate(query_parts):
        total_ref[:, pl.ds(head * rows, rows)] = part


def pair_kernel(
    offset, window, heads, last, key_value_ref, query_ref, grad_ref, mix_ref, norm_ref, delta_ref,
    before_ref, total_ref, sums_ref,
):
    rows, width = key_value_ref.shape[0] // 2, key_value_ref.shape[1]
    grad_scale = keep_scale * width**-0.5
    key_sum, value_sum, query_parts = block_grads(
        offset, window, heads, key_value_ref[:rows], key_value_ref[rows:], query_ref, grad_ref,
        mix_ref, norm_ref, delta_ref,
    )
    sums_ref[:rows] = (key_sum * f32(grad_scale)).astype(bf16)
    sums_ref[rows:] = (value_sum * f32(keep_scale)).astype(bf16)
    for head, part in enumerate(query_parts):
        cols = pl.ds(head * rows, rows)
        if last:
            total_ref[:, pl.ds(head * width, width)] = (
                (before_ref[:, cols] + part).T * f32(grad_scale)
            ).astype(bf16)
        else:
            total_ref[:, cols] = before_ref[:, cols] + part


def project_kernel(hop, flip, start, added, query_ref, sums_ref, wq_ref, wk_ref, wv_ref, *refs):
    count = lax.axis_size("tp")
    me = lax.axis_index("tp")
    if flip:
        me = me + 1 - 2 * lax.rem(me, 2)
    out_ref = refs[-1]
    rows, cols = out_ref.shape
    first = lax.rem(me + hop, count) * (wq_ref.shape[0] // count) + start
    at = pl.ds(pl.multiple_of(first, 128), cols)
    total = dot(query_ref[...], wq_ref[at, :], 1, 1)
    total = total + dot(sums_ref[:rows], wk_ref[at, :], 1, 1)
    total = total + dot(sums_ref[rows:], wv_ref[at, :], 1, 1)
    for ref in refs[:added]:
        total = total + ref[...].astype(f32)
    out_ref[...] = total.astype(out_ref.dtype)


def project(hop, flip, start, cols, operands, added, after, dtype, params):
    rows, depth = operands[0].shape[0], sum(item.shape[1] for item in operands[2:])
    return pl.pallas_call(
        functools.partial(project_kernel, hop, flip, start, len(added)),
        in_specs=[in_vmem] * (len(operands) + len(added) + len(after)),
        out_specs=in_vmem,
        out_shape=jax.ShapeDtypeStruct((rows, cols), dtype),
        compiler_params=params,
        cost_estimate=cost(2 * rows * cols * depth),
        name="project",
    )(*operands, *added, *after)


def add_kernel(left_ref, right_ref, out_ref):
    out_ref[...] = (left_ref[...] + right_ref[...].astype(f32)).astype(out_ref.dtype)


def finish_kernel(first, hops, mine_ref, *refs):
    out_hbm, held, sem = refs[-3:]
    at = pl.ds(first, held.shape[1])
    total = mine_ref[:, at]
    for ref in refs[:hops]:
        total = total + ref[...].astype(f32)
    held[...] = total.astype(bf16)
    copy = pltpu.make_async_copy(held, out_hbm.at[:, at], sem)
    copy.start()
    copy.wait()


def cost(flops):
    return pl.CostEstimate(flops=flops, bytes_accessed=flops // 400, transcendentals=0)


def on_device(
    queries,
    keys,
    values,
    outputs,
    out_grad,
    log_norm,
    block_mask,
    counter_base,
    q_weight,
    k_weight,
    v_weight,
):
    rows, width = keys.shape
    heads = log_norm.shape[1]
    steps = block_mask.shape[1]
    window = 3 * rows + rows // 2
    tp_size = lax.axis_size("tp")
    params = pltpu.CompilerParams(vmem_limit_bytes=16 * 2**20)

    shape = jax.ShapeDtypeStruct
    key_value, query, grad, output, mix, norms = pl.pallas_call(
        functools.partial(load_kernel, heads),
        in_specs=[in_hbm] * 8,
        out_specs=[in_vmem] * 6,
        out_shape=[
            shape((2 * rows, width), bf16),
            *[shape(queries.shape, bf16)] * 3,
            shape((heads, rows), i32),
            shape((steps * heads, rows), f32),
        ],
        scratch_shapes=[
            pltpu.VMEM((heads, rows), f32),
            pltpu.SMEM(counter_base.shape, i32),
            pltpu.SMEM(block_mask.shape, i32),
            pltpu.SemaphoreType.DMA((8,)),
        ],
        compiler_params=params,
        cost_estimate=pl.CostEstimate(flops=0, bytes_accessed=0, transcendentals=0),
        name="load",
    )(*map(from_hbm, (keys, values, queries, out_grad, outputs, log_norm.T, counter_base, block_mask)))
    order = range(steps - 1, 0, -1)
    arrived = {offset: cyclic(key_value, "ctx", offset) for offset in order}
    block_cost = cost(20 * heads * rows * rows * width)

    deltas, total, own_sums = pl.pallas_call(
        functools.partial(own_kernel, window, heads),
        in_specs=[in_vmem] * 6,
        out_specs=[in_vmem] * 3,
        out_shape=[
            shape((heads, rows), f32),
            shape((width, heads * rows), f32),
            shape((2 * rows, width), f32),
        ],
        compiler_params=params,
        cost_estimate=block_cost,
        name="own_block",
    )(key_value, query, grad, output, mix, norms)

    returned = []
    for offset in order:
        last = offset == order[-1]
        total, sums = pl.pallas_call(
            functools.partial(pair_kernel, offset, window, heads, last),
            in_specs=[in_vmem] * 7,
            out_specs=[in_vmem] * 2,
            out_shape=[
                shape((rows, heads * width), bf16) if last else shape((width, heads * rows), f32),
                shape((2 * rows, width), bf16),
            ],
            compiler_params=params,
            cost_estimate=block_cost,
            name="block_back_%d" % offset,
        )(arrived[offset], query, grad, mix, norms, deltas, total)
        returned.append(cyclic(sums, "ctx", -offset))
    grad_query = total
    sums = own_sums
    for item in returned:
        sums = pl.pallas_call(
            add_kernel,
            in_specs=[in_vmem] * 2,
            out_specs=in_vmem,
            out_shape=shape(sums.shape, bf16 if item is returned[-1] else f32),
            compiler_params=params,
            cost_estimate=block_cost,
            name="add_returned",
        )(sums, item)
    operands = (grad_query, sums, q_weight, k_weight, v_weight)
    cols = q_weight.shape[0] // tp_size
    sizes = [cols // 2] * 2
    starts = [sum(sizes[:i]) for i in range(len(sizes))]
    hops = tp_size // 2 - 1
    places = [(i, hop) for i in range(len(sizes)) for hop in range(2, tp_size, 2)]
    swapped, terms, after = [], [], ()
    for i, hop in places:
        part = project(hop, True, starts[i], sizes[i], operands, (), after, bf16, params)
        swapped.append(other_core(part))
        after = (part,)
    for (i, hop), item in zip(places, swapped):
        part = project(hop, False, starts[i], sizes[i], operands, (item,), after, bf16, params)
        terms.append(part)
        after = (part,)
        if len(terms) == 1:
            part = project(0, True, 0, cols, operands, (), after, bf16, params)
            other = other_core(part)
            after = (part,)
    sent = [cyclic(term, "tp", hop) for (_, hop), term in zip(places, terms)]
    mine = project(0, False, 0, cols, operands, (other,), tuple(sent[:1]), f32, params)
    out = ()
    for i, size in enumerate(sizes):
        out = pl.pallas_call(
            functools.partial(finish_kernel, starts[i], hops),
            in_specs=[in_vmem] * (1 + hops) + [in_hbm] * len(out),
            out_specs=in_hbm,
            out_shape=shape((rows, cols), bf16),
            input_output_aliases={1 + hops: 0} if out else {},
            scratch_shapes=[pltpu.VMEM((rows, size), bf16), pltpu.SemaphoreType.DMA],
            compiler_params=params,
            cost_estimate=cost(10**6),
            name="finish",
        )(mine, *sent[i * hops : (i + 1) * hops], *out)
        out = (out,)
    return out[0]


def solution(mesh):
    return jax.shard_map(
        on_device,
        mesh=mesh,
        in_specs=(
            P("ctx", "tp"),
            P("ctx", "tp"),
            P("ctx", "tp"),
            P("ctx", "tp"),
            P("ctx", "tp"),
            P("ctx", "tp"),
            P("ctx", None),
            P(),
            P(None, "tp"),
            P(None, "tp"),
            P(None, "tp"),
        ),
        out_specs=P("ctx", "tp"),
        check_vma=False,
    )
```

```python
import functools
import math

import jax
import jax.numpy as jnp
from jax import lax
from jax.experimental import pallas as pl
from jax.experimental.pallas import tpu as pltpu
from jax.sharding import PartitionSpec as P

keep_level = 103
keep_scale = 1024.0 / 921.0
log2_e = math.log2(math.e)
f32, bf16, i32 = jnp.float32, jnp.bfloat16, jnp.int32
in_vmem = pl.BlockSpec(memory_space=pltpu.VMEM)
in_hbm = pl.BlockSpec(memory_space=pltpu.HBM)
in_smem = pl.BlockSpec(memory_space=pltpu.SMEM)


def from_hbm(array):
    return pltpu.with_memory_space_constraint(array, pltpu.HBM)


def moved(array, axis, place):
    count = lax.axis_size(axis)
    return lax.ppermute(array, axis, [(i, place(i) % count) for i in range(count)])


def other_core(array):
    return moved(array, "tp", lambda i: i ^ 1)


def by_parity(even, odd):
    return jnp.where(lax.rem(lax.axis_index("ctx"), 2) == 1, odd, even)


def dot(left, right, left_dim, right_dim):
    return lax.dot_general(
        left, right, (((left_dim,), (right_dim,)), ((), ())), preferred_element_type=f32
    )


def keep_mask(mixed):
    mixed = mixed ^ lax.shift_right_logical(mixed, i32(15))
    mixed = mixed * i32(739982445)
    mixed = mixed ^ lax.shift_right_logical(mixed, i32(12))
    mixed = mixed * i32(695872825)
    mixed = mixed ^ lax.shift_right_logical(mixed, i32(15))
    return (mixed & i32(1023)) >= i32(keep_level)


def block_grads(offsets, window, heads, key, value, query_ref, grad_ref, mix_ref, norm_ref, delta_ref):
    rows, width = key.shape
    offset = offsets[0] if offsets[0] == offsets[1] else by_parity(*offsets)
    key_index = lax.broadcasted_iota(i32, (rows, rows), 0)
    query_index = lax.broadcasted_iota(i32, (rows, rows), 1)
    key_part = (key_index - offset * rows) * i32(19349663)
    key_t = key.T
    scale = log2_e * width**-0.5
    key_sum = value_sum = None
    query_parts = []
    for head in range(heads):
        cols = pl.ds(head * width, width)
        query, grad = query_ref[:, cols], grad_ref[:, cols]
        log_norm = norm_ref[pl.ds(offset * heads + head, 1), :]
        row_delta = delta_ref[pl.ds(head, 1), :]
        kept = keep_mask(key_part + mix_ref[pl.ds(head, 1), :])
        probs = jnp.exp2(dot(key, query, 1, 1) * scale - log_norm)
        spacing = query_index - key_index
        if 0 in offsets:
            probs = jnp.where(spacing >= 0, probs, f32(0.0))
        if (max(offsets) + 1) * rows > window:
            probs = jnp.where(spacing < window - offset * rows, probs, f32(0.0))
        dropped = jnp.where(kept, probs, f32(0.0)).astype(bf16)
        grad_probs = dot(value, grad, 1, 1)
        grad_scores = (
            probs * (jnp.where(kept, grad_probs, f32(0.0)) - row_delta)
        ).astype(bf16)
        value_add = dot(dropped, grad, 1, 0)
        key_add = dot(grad_scores, query, 1, 0)
        key_sum = key_add if head == 0 else key_sum + key_add
        value_sum = value_add if head == 0 else value_sum + value_add
        query_parts.append(dot(key_t, grad_scores, 1, 0))
    return key_sum, value_sum, query_parts


def load_kernel(
    heads, key_hbm, value_hbm, query_hbm, grad_hbm, output_hbm, norm_hbm, counter_hbm, mask_hbm,
    key_value, query, grad, output, mix_ref, rows_ref, norm_ref, counter_ref, mask_ref, sems,
):
    rows = key_hbm.shape[0]
    copies = [
        pltpu.make_async_copy(source, target, sems.at[i])
        for i, (source, target) in enumerate(
            (
                (key_hbm, key_value.at[pl.ds(0, rows)]),
                (value_hbm, key_value.at[pl.ds(rows, rows)]),
                (counter_hbm, counter_ref),
                (mask_hbm, mask_ref),
                (norm_hbm, norm_ref),
                (query_hbm, query),
                (grad_hbm, grad),
                (output_hbm, output),
            )
        )
    ]
    for copy in copies:
        copy.start()
    for copy in copies:
        copy.wait()
    block_id = lax.axis_index("ctx")
    first_head = lax.axis_index("tp") * heads
    base = counter_ref[1] + block_id * rows
    common = base * i32(19349663) + counter_ref[0]
    query_pos = lax.broadcasted_iota(i32, (1, rows), 1) + base
    for head in range(heads):
        mix_ref[pl.ds(head, 1), :] = query_pos * i32(73856093) + (
            common + (first_head + head) * i32(83492791)
        )
    norms = norm_ref[...] * f32(log2_e)
    for offset in range(mask_ref.shape[1]):
        active = (block_id >= offset) & (mask_ref[0, offset] == 1)
        rows_ref[pl.ds(offset * heads, heads), :] = jnp.where(active, norms, f32(jnp.inf))


def with_copies(loads, results, refs):
    copies = []
    for i, (start, size) in enumerate(loads):
        source = refs[i]
        copies.append(pltpu.make_async_copy(source, refs[len(loads) + results + i], refs[-1].at[i]))
        copies[-1].start()
    return refs[len(loads) : len(loads) + results], copies


def own_kernel(
    window, heads, loads, key_value_ref, query_ref, grad_ref, output_ref, mix_ref, norm_ref, *refs
):
    (delta_ref, total_ref, sums_ref), copies = with_copies(loads, 3, refs)
    rows, width = key_value_ref.shape[0] // 2, key_value_ref.shape[1]
    lane = lax.broadcasted_iota(i32, (rows, 128), 1)
    packed = jnp.zeros((rows, 128), f32)
    for head in range(heads):
        cols = pl.ds(head * width, width)
        delta = jnp.sum(
            grad_ref[:, cols].astype(f32) * output_ref[:, cols].astype(f32), axis=1, keepdims=True
        )
        packed = jnp.where(lane == head, delta * f32(1.0 / keep_scale), packed)
    delta_ref[...] = packed.T[: delta_ref.shape[0]]
    key_sum, value_sum, query_parts = block_grads(
        (0, 0), window, heads, key_value_ref[:rows], key_value_ref[rows:], query_ref, grad_ref, mix_ref,
        norm_ref, delta_ref,
    )
    grad_scale = keep_scale * width**-0.5
    sums_ref[:rows] = key_sum * f32(grad_scale)
    sums_ref[rows:] = value_sum * f32(keep_scale)
    for head, part in enumerate(query_parts):
        total_ref[:, pl.ds(head * rows, rows)] = part
    for copy in copies:
        copy.wait()


def pair_kernel(
    offsets, window, heads, loads, last, key_value_ref, query_ref, grad_ref, mix_ref, norm_ref, delta_ref,
    before_ref, *refs,
):
    (total_ref, sums_ref), copies = with_copies(loads, 2, refs)
    rows, width = key_value_ref.shape[0] // 2, key_value_ref.shape[1]
    grad_scale = keep_scale * width**-0.5
    key_sum, value_sum, query_parts = block_grads(
        offsets, window, heads, key_value_ref[:rows], key_value_ref[rows:], query_ref, grad_ref,
        mix_ref, norm_ref, delta_ref,
    )
    sums_ref[:rows] = (key_sum * f32(grad_scale)).astype(bf16)
    sums_ref[rows:] = (value_sum * f32(keep_scale)).astype(bf16)
    for head, part in enumerate(query_parts):
        cols = pl.ds(head * rows, rows)
        if last:
            total_ref[:, pl.ds(head * width, width)] = (
                (before_ref[:, cols] + part).T * f32(grad_scale)
            ).astype(bf16)
        else:
            total_ref[:, cols] = before_ref[:, cols] + part
    for copy in copies:
        copy.wait()


def query_term_kernel(query_ref, wq_ref, out_ref):
    places, _, cols = out_ref.shape
    query = query_ref[...]
    for place in range(places):
        out_ref[place] = dot(query, wq_ref[pl.ds(place * cols, cols), :], 1, 1)


def term_kernel(pieces, added, sums_ref, term_ref, wk_ref, wv_ref, *refs):
    count, rows, block = term_ref.shape
    me = lax.axis_index("tp")
    out_ref = refs[-1]
    keys, values = sums_ref[:rows], sums_ref[rows:]
    done = 0
    for hop, flip, start, cols in pieces:
        place = lax.rem((me + 1 - 2 * lax.rem(me, 2) if flip else me) + hop, count)
        at = pl.ds(pl.multiple_of(place * block + start, 128), cols)
        total = term_ref[place, :, pl.ds(start, cols)]
        total = total + dot(keys, wk_ref[at, :], 1, 1) + dot(values, wv_ref[at, :], 1, 1)
        if added is not None:
            total = total + refs[0][:, pl.ds(added + done, cols)].astype(f32)
        out_ref[:, pl.ds(done, cols)] = total.astype(out_ref.dtype)
        done += cols


def term(pieces, operands, added, after, dtype, flops, params):
    rows = operands[1].shape[1]
    first, extra = (None, ()) if added is None else (added[1], added[:1])
    return pl.pallas_call(
        functools.partial(term_kernel, pieces, first),
        in_specs=[in_vmem] * (len(operands) + len(extra) + len(after)),
        out_specs=in_vmem,
        out_shape=jax.ShapeDtypeStruct((rows, sum(piece[3] for piece in pieces)), dtype),
        compiler_params=params,
        cost_estimate=cost(flops),
        name="term",
    )(*operands, *extra, *after)


def add_kernel(left_ref, right_ref, *refs):
    out_ref = refs[-1]
    out_ref[...] = (left_ref[...] + right_ref[...].astype(f32)).astype(out_ref.dtype)


def finish_kernel(first, hops, low_ref, high_ref, *refs):
    out_hbm, held, sem = refs[-3:]
    half, size = low_ref.shape[1], held.shape[1]
    for start in range(first, first + size, 128):
        ref, at = (low_ref, start) if start < half else (high_ref, start - half)
        total = ref[:, pl.ds(at, 128)]
        for ref in refs[:hops]:
            total = total + ref[:, pl.ds(start - first, 128)].astype(f32)
        held[:, pl.ds(start - first, 128)] = total.astype(bf16)
    copy = pltpu.make_async_copy(held, out_hbm.at[:, pl.ds(first, size)], sem)
    copy.start()
    copy.wait()


def cost(flops):
    return pl.CostEstimate(flops=flops, bytes_accessed=flops // 400, transcendentals=0)


def on_device(
    queries,
    keys,
    values,
    outputs,
    out_grad,
    log_norm,
    block_mask,
    counter_base,
    q_weight,
    k_weight,
    v_weight,
):
    rows, width = keys.shape
    heads = log_norm.shape[1]
    steps = block_mask.shape[1]
    window = 3 * rows + rows // 2
    tp_size = lax.axis_size("tp")
    params = pltpu.CompilerParams(vmem_limit_bytes=16 * 2**20)

    shape = jax.ShapeDtypeStruct
    key_value, query, grad, output, mix, norms = pl.pallas_call(
        functools.partial(load_kernel, heads),
        in_specs=[in_hbm] * 8,
        out_specs=[in_vmem] * 6,
        out_shape=[
            shape((2 * rows, width), bf16),
            *[shape(queries.shape, bf16)] * 3,
            shape((heads, rows), i32),
            shape((steps * heads, rows), f32),
        ],
        scratch_shapes=[
            pltpu.VMEM((heads, rows), f32),
            pltpu.SMEM(counter_base.shape, i32),
            pltpu.SMEM(block_mask.shape, i32),
            pltpu.SemaphoreType.DMA((8,)),
        ],
        compiler_params=params,
        cost_estimate=pl.CostEstimate(flops=0, bytes_accessed=0, transcendentals=0),
        name="load",
    )(*map(from_hbm, (keys, values, queries, out_grad, outputs, log_norm.T, counter_base, block_mask)))
    straight = moved(key_value, "ctx", lambda i: i + 2)
    mixed = moved(key_value, "ctx", lambda i: i + 3 if i % 2 else i + 1)
    block_cost = cost(20 * heads * rows * rows * width)

    all_rows = (0, q_weight.shape[0])
    loads = (
        ((q_weight,), (all_rows,)),
        ((k_weight, v_weight), (all_rows,) * 2),
        ((), ()),
        ((), ()),
    )

    def loaded(load):
        return [shape((size, item.shape[1]), bf16) for item, (_, size) in zip(*load)]

    deltas, total, sums, *q_low = pl.pallas_call(
        functools.partial(own_kernel, window, heads, loads[0][1]),
        in_specs=[in_vmem] * 6 + [in_hbm] * len(loads[0][0]),
        out_specs=[in_vmem] * (3 + len(loads[0][0])),
        out_shape=[
            shape((heads, rows), f32),
            shape((width, heads * rows), f32),
            shape((2 * rows, width), f32),
            *loaded(loads[0]),
        ],
        scratch_shapes=[pltpu.SemaphoreType.DMA((len(loads[0][0]),))],
        compiler_params=params,
        cost_estimate=cost(10**6),
        name="own_block",
    )(key_value, query, grad, output, mix, norms, *map(from_hbm, loads[0][0]))

    straight, deltas = lax.optimization_barrier((straight, deltas))
    crossed = moved(straight, "ctx", lambda i: i ^ 1)
    returned, held = [], [*q_low]
    for load, offsets, arrived in zip(
        loads[1:], ((2, 2), (3, 1), (1, 3)), (straight, mixed, crossed)
    ):
        last = offsets == (1, 3)
        total, parts, *more = pl.pallas_call(
            functools.partial(pair_kernel, offsets, window, heads, load[1], last),
            in_specs=[in_vmem] * 7 + [in_hbm] * len(load[0]),
            out_specs=[in_vmem] * (2 + len(load[0])),
            out_shape=[
                shape((rows, heads * width), bf16) if last else shape((width, heads * rows), f32),
                shape((2 * rows, width), bf16),
                *loaded(load),
            ],
            scratch_shapes=[pltpu.SemaphoreType.DMA((len(load[0]),))] * (len(load[0]) > 0),
            compiler_params=params,
            cost_estimate=cost(10**6),
            name="block_back_%d%d" % offsets,
        )(arrived, query, grad, mix, norms, deltas, total, *map(from_hbm, load[0]))
        held.extend(more)
        even, odd = offsets
        returned.append(moved(parts, "ctx", lambda i: i - (odd if i % 2 else even)))

    cols = q_weight.shape[0] // tp_size
    query_term = pl.pallas_call(
        query_term_kernel,
        in_specs=[in_vmem] * 2,
        out_specs=in_vmem,
        out_shape=shape((tp_size, rows, cols), f32),
        compiler_params=params,
        cost_estimate=block_cost,
        name="query_term",
    )(total, held[0])
    for item in returned:
        final = item is returned[-1]
        sums = pl.pallas_call(
            add_kernel,
            in_specs=[in_vmem] * (3 if final else 2),
            out_specs=in_vmem,
            out_shape=shape(sums.shape, bf16 if final else f32),
            compiler_params=params,
            cost_estimate=block_cost,
            name="add_returned",
        )(sums, item, *((query_term,) if final else ()))

    operands = (sums, query_term, *held[1:])
    hops = range(2, tp_size, 2)
    sizes = (cols * 5 // 8, cols * 3 // 8) if cols % 1024 == 0 else (cols // 2,) * 2
    starts = (0, sizes[0])
    low, high = 10**6, block_cost.flops

    def swapped_term(places, after):
        pieces = [(hop, True, start, size) for hop, start, size in places]
        part = term(pieces, operands, None, after, bf16, low, params)
        return part, other_core(part)

    swapped, after = [], ()
    for i in range(2):
        part, item = swapped_term([(hop, starts[i], sizes[i]) for hop in hops], after)
        swapped.append(item)
        after = (part,)
    part, swapped_low = swapped_term([(0, 0, cols // 2)], after)
    part, swapped_high = swapped_term([(0, cols // 2, cols // 2)], (part,))
    sent, after = [[], []], (part,)
    for i in range(2):
        for j, hop in enumerate(hops):
            piece = ((hop, False, starts[i], sizes[i]),)
            part = term(piece, operands, (swapped[i], j * sizes[i]), after, bf16, low, params)
            sent[i].append(moved(part, "tp", lambda k: k + hop))
            after = (part,)
    mine = [
        term(((0, False, j * (cols // 2), cols // 2),), operands, (item, 0), tuple(sent[0][:1]), f32, 10 * high, params)
        for j, item in enumerate((swapped_low, swapped_high))
    ]
    out = ()
    for i in range(2):
        out = pl.pallas_call(
            functools.partial(finish_kernel, starts[i], len(hops)),
            in_specs=[in_vmem] * (2 + len(hops)) + [in_hbm] * len(out),
            out_specs=in_hbm,
            out_shape=shape((rows, cols), bf16),
            input_output_aliases={2 + len(hops): 0} if out else {},
            scratch_shapes=[pltpu.VMEM((rows, sizes[i]), bf16), pltpu.SemaphoreType.DMA],
            compiler_params=params,
            cost_estimate=cost(low),
            name="finish",
        )(*mine, *sent[i], *out)
        out = (out,)
    return out[0]


def solution(mesh):
    return jax.shard_map(
        on_device,
        mesh=mesh,
        in_specs=(
            P("ctx", "tp"),
            P("ctx", "tp"),
            P("ctx", "tp"),
            P("ctx", "tp"),
            P("ctx", "tp"),
            P("ctx", "tp"),
            P("ctx", None),
            P(),
            P(None, "tp"),
            P(None, "tp"),
            P(None, "tp"),
        ),
        out_specs=P("ctx", "tp"),
        check_vma=False,
    )
```

```python
import functools
import math

import jax
import jax.numpy as jnp
from jax import lax
from jax.experimental import pallas as pl
from jax.experimental.pallas import tpu as pltpu
from jax.sharding import PartitionSpec as P

keep_level = 103
keep_scale = 1024.0 / 921.0
log2_e = math.log2(math.e)
f32, bf16, i32 = jnp.float32, jnp.bfloat16, jnp.int32
in_vmem = pl.BlockSpec(memory_space=pltpu.VMEM)
in_hbm = pl.BlockSpec(memory_space=pltpu.HBM)
in_smem = pl.BlockSpec(memory_space=pltpu.SMEM)


def from_hbm(array):
    return pltpu.with_memory_space_constraint(array, pltpu.HBM)


def moved(array, axis, place):
    count = lax.axis_size(axis)
    return lax.ppermute(array, axis, [(i, place(i) % count) for i in range(count)])


def other_core(array):
    return moved(array, "tp", lambda i: i ^ 1)


def by_parity(even, odd):
    return jnp.where(lax.rem(lax.axis_index("ctx"), 2) == 1, odd, even)


def dot(left, right, left_dim, right_dim):
    return lax.dot_general(
        left, right, (((left_dim,), (right_dim,)), ((), ())), preferred_element_type=f32
    )


def keep_mask(mixed):
    mixed = mixed ^ lax.shift_right_logical(mixed, i32(15))
    mixed = mixed * i32(739982445)
    mixed = mixed ^ lax.shift_right_logical(mixed, i32(12))
    mixed = mixed * i32(695872825)
    mixed = mixed ^ lax.shift_right_logical(mixed, i32(15))
    return (mixed & i32(1023)) >= i32(keep_level)


def block_grads(offsets, window, heads, key, value, query_ref, grad_ref, mix_ref, norm_ref, delta_ref):
    rows, width = key.shape
    offset = offsets[0] if offsets[0] == offsets[1] else by_parity(*offsets)
    key_index = lax.broadcasted_iota(i32, (rows, rows), 0)
    query_index = lax.broadcasted_iota(i32, (rows, rows), 1)
    key_part = (key_index - offset * rows) * i32(19349663)
    key_t = key.T
    scale = log2_e * width**-0.5
    key_sum = value_sum = None
    query_parts = []
    for head in range(heads):
        cols = pl.ds(head * width, width)
        query, grad = query_ref[:, cols], grad_ref[:, cols]
        log_norm = norm_ref[pl.ds(offset * heads + head, 1), :]
        row_delta = delta_ref[pl.ds(head, 1), :]
        kept = keep_mask(key_part + mix_ref[pl.ds(head, 1), :])
        probs = jnp.exp2(dot(key, query, 1, 1) * scale - log_norm)
        spacing = query_index - key_index
        if 0 in offsets:
            probs = jnp.where(spacing >= 0, probs, f32(0.0))
        if (max(offsets) + 1) * rows > window:
            probs = jnp.where(spacing < window - offset * rows, probs, f32(0.0))
        dropped = jnp.where(kept, probs, f32(0.0)).astype(bf16)
        grad_probs = dot(value, grad, 1, 1)
        grad_scores = (
            probs * (jnp.where(kept, grad_probs, f32(0.0)) - row_delta)
        ).astype(bf16)
        value_add = dot(dropped, grad, 1, 0)
        key_add = dot(grad_scores, query, 1, 0)
        key_sum = key_add if head == 0 else key_sum + key_add
        value_sum = value_add if head == 0 else value_sum + value_add
        query_parts.append(dot(key_t, grad_scores, 1, 0))
    return key_sum, value_sum, query_parts


def load_kernel(
    heads, key_hbm, value_hbm, query_hbm, grad_hbm, output_hbm, norm_hbm, counter_hbm, mask_hbm,
    key_value, query, grad, output, mix_ref, rows_ref, norm_ref, counter_ref, mask_ref, sems,
):
    rows = key_hbm.shape[0]
    copies = [
        pltpu.make_async_copy(source, target, sems.at[i])
        for i, (source, target) in enumerate(
            (
                (key_hbm, key_value.at[pl.ds(0, rows)]),
                (value_hbm, key_value.at[pl.ds(rows, rows)]),
                (counter_hbm, counter_ref),
                (mask_hbm, mask_ref),
                (norm_hbm, norm_ref),
                (query_hbm, query),
                (grad_hbm, grad),
                (output_hbm, output),
            )
        )
    ]
    for copy in copies:
        copy.start()
    for copy in copies:
        copy.wait()
    block_id = lax.axis_index("ctx")
    first_head = lax.axis_index("tp") * heads
    base = counter_ref[1] + block_id * rows
    common = base * i32(19349663) + counter_ref[0]
    query_pos = lax.broadcasted_iota(i32, (1, rows), 1) + base
    for head in range(heads):
        mix_ref[pl.ds(head, 1), :] = query_pos * i32(73856093) + (
            common + (first_head + head) * i32(83492791)
        )
    norms = norm_ref[...] * f32(log2_e)
    for offset in range(mask_ref.shape[1]):
        active = (block_id >= offset) & (mask_ref[0, offset] == 1)
        rows_ref[pl.ds(offset * heads, heads), :] = jnp.where(active, norms, f32(jnp.inf))


def with_copies(loads, results, refs):
    copies = []
    for i, (start, size) in enumerate(loads):
        source = refs[i]
        copies.append(pltpu.make_async_copy(source, refs[len(loads) + results + i], refs[-1].at[i]))
        copies[-1].start()
    return refs[len(loads) : len(loads) + results], copies


def own_kernel(
    window, heads, loads, key_value_ref, query_ref, grad_ref, output_ref, mix_ref, norm_ref, *refs
):
    (delta_ref, total_ref, sums_ref), copies = with_copies(loads, 3, refs)
    rows, width = key_value_ref.shape[0] // 2, key_value_ref.shape[1]
    lane = lax.broadcasted_iota(i32, (rows, 128), 1)
    packed = jnp.zeros((rows, 128), f32)
    for head in range(heads):
        cols = pl.ds(head * width, width)
        delta = jnp.sum(
            grad_ref[:, cols].astype(f32) * output_ref[:, cols].astype(f32), axis=1, keepdims=True
        )
        packed = jnp.where(lane == head, delta * f32(1.0 / keep_scale), packed)
    delta_ref[...] = packed.T[: delta_ref.shape[0]]
    key_sum, value_sum, query_parts = block_grads(
        (0, 0), window, heads, key_value_ref[:rows], key_value_ref[rows:], query_ref, grad_ref, mix_ref,
        norm_ref, delta_ref,
    )
    grad_scale = keep_scale * width**-0.5
    sums_ref[:rows] = key_sum * f32(grad_scale)
    sums_ref[rows:] = value_sum * f32(keep_scale)
    for head, part in enumerate(query_parts):
        total_ref[:, pl.ds(head * rows, rows)] = part
    for copy in copies:
        copy.wait()


def pair_kernel(
    offsets, window, heads, loads, last, key_value_ref, query_ref, grad_ref, mix_ref, norm_ref, delta_ref,
    before_ref, *refs,
):
    (total_ref, sums_ref), copies = with_copies(loads, 2, refs)
    rows, width = key_value_ref.shape[0] // 2, key_value_ref.shape[1]
    grad_scale = keep_scale * width**-0.5
    key_sum, value_sum, query_parts = block_grads(
        offsets, window, heads, key_value_ref[:rows], key_value_ref[rows:], query_ref, grad_ref,
        mix_ref, norm_ref, delta_ref,
    )
    sums_ref[:rows] = (key_sum * f32(grad_scale)).astype(bf16)
    sums_ref[rows:] = (value_sum * f32(keep_scale)).astype(bf16)
    for head, part in enumerate(query_parts):
        cols = pl.ds(head * rows, rows)
        if last:
            total_ref[:, pl.ds(head * width, width)] = (
                (before_ref[:, cols] + part).T * f32(grad_scale)
            ).astype(bf16)
        else:
            total_ref[:, cols] = before_ref[:, cols] + part
    for copy in copies:
        copy.wait()


def query_term_kernel(query_ref, wq_ref, out_ref):
    places, _, cols = out_ref.shape
    query = query_ref[...]
    for place in range(places):
        out_ref[place] = dot(query, wq_ref[pl.ds(place * cols, cols), :], 1, 1)


def term_kernel(pieces, added, sums_ref, term_ref, wk_ref, wv_ref, *refs):
    count, rows, block = term_ref.shape
    me = lax.axis_index("tp")
    out_ref = refs[-1]
    keys, values = sums_ref[:rows], sums_ref[rows:]
    done = 0
    for hop, flip, start, cols in pieces:
        place = lax.rem((me + 1 - 2 * lax.rem(me, 2) if flip else me) + hop, count)
        at = pl.ds(pl.multiple_of(place * block + start, 128), cols)
        total = term_ref[place, :, pl.ds(start, cols)]
        total = total + dot(keys, wk_ref[at, :], 1, 1) + dot(values, wv_ref[at, :], 1, 1)
        if added is not None:
            total = total + refs[0][:, pl.ds(added + done, cols)].astype(f32)
        out_ref[:, pl.ds(done, cols)] = total.astype(out_ref.dtype)
        done += cols


def term(pieces, operands, added, after, dtype, flops, params):
    rows = operands[1].shape[1]
    first, extra = (None, ()) if added is None else (added[1], added[:1])
    return pl.pallas_call(
        functools.partial(term_kernel, pieces, first),
        in_specs=[in_vmem] * (len(operands) + len(extra) + len(after)),
        out_specs=in_vmem,
        out_shape=jax.ShapeDtypeStruct((rows, sum(piece[3] for piece in pieces)), dtype),
        compiler_params=params,
        cost_estimate=cost(flops),
        name="term",
    )(*operands, *extra, *after)


def add_kernel(left_ref, right_ref, *refs):
    out_ref = refs[-1]
    out_ref[...] = (left_ref[...] + right_ref[...].astype(f32)).astype(out_ref.dtype)


def finish_kernel(first, hops, low_ref, high_ref, *refs):
    out_hbm, held, sem = refs[-3:]
    half, size = low_ref.shape[1], held.shape[1]
    for start in range(first, first + size, 128):
        ref, at = (low_ref, start) if start < half else (high_ref, start - half)
        total = ref[:, pl.ds(at, 128)]
        for ref in refs[:hops]:
            total = total + ref[:, pl.ds(start - first, 128)].astype(f32)
        held[:, pl.ds(start - first, 128)] = total.astype(bf16)
    copy = pltpu.make_async_copy(held, out_hbm.at[:, pl.ds(first, size)], sem)
    copy.start()
    copy.wait()


def cost(flops):
    return pl.CostEstimate(flops=flops, bytes_accessed=flops // 400, transcendentals=0)


def on_device(
    queries,
    keys,
    values,
    outputs,
    out_grad,
    log_norm,
    block_mask,
    counter_base,
    q_weight,
    k_weight,
    v_weight,
):
    rows, width = keys.shape
    heads = log_norm.shape[1]
    steps = block_mask.shape[1]
    window = 3 * rows + rows // 2
    tp_size = lax.axis_size("tp")
    params = pltpu.CompilerParams(vmem_limit_bytes=16 * 2**20)

    shape = jax.ShapeDtypeStruct
    key_value, query, grad, output, mix, norms = pl.pallas_call(
        functools.partial(load_kernel, heads),
        in_specs=[in_hbm] * 8,
        out_specs=[in_vmem] * 6,
        out_shape=[
            shape((2 * rows, width), bf16),
            *[shape(queries.shape, bf16)] * 3,
            shape((heads, rows), i32),
            shape((steps * heads, rows), f32),
        ],
        scratch_shapes=[
            pltpu.VMEM((heads, rows), f32),
            pltpu.SMEM(counter_base.shape, i32),
            pltpu.SMEM(block_mask.shape, i32),
            pltpu.SemaphoreType.DMA((8,)),
        ],
        compiler_params=params,
        cost_estimate=pl.CostEstimate(flops=0, bytes_accessed=0, transcendentals=0),
        name="load",
    )(*map(from_hbm, (keys, values, queries, out_grad, outputs, log_norm.T, counter_base, block_mask)))
    straight = moved(key_value, "ctx", lambda i: i + 2)
    count = lax.axis_size("ctx")
    pairs = [(i, i + (3 if i % 2 else 1)) for i in range(count)]
    mixed = lax.ppermute(key_value, "ctx", [pair for pair in pairs if pair[1] < count])
    block_cost = cost(20 * heads * rows * rows * width)

    all_rows = (0, q_weight.shape[0])
    loads = (
        ((q_weight,), (all_rows,)),
        ((k_weight, v_weight), (all_rows,) * 2),
        ((), ()),
        ((), ()),
    )

    def loaded(load):
        return [shape((size, item.shape[1]), bf16) for item, (_, size) in zip(*load)]

    deltas, total, sums, *q_low = pl.pallas_call(
        functools.partial(own_kernel, window, heads, loads[0][1]),
        in_specs=[in_vmem] * 6 + [in_hbm] * len(loads[0][0]),
        out_specs=[in_vmem] * (3 + len(loads[0][0])),
        out_shape=[
            shape((heads, rows), f32),
            shape((width, heads * rows), f32),
            shape((2 * rows, width), f32),
            *loaded(loads[0]),
        ],
        scratch_shapes=[pltpu.SemaphoreType.DMA((len(loads[0][0]),))],
        compiler_params=params,
        cost_estimate=cost(10**6),
        name="own_block",
    )(key_value, query, grad, output, mix, norms, *map(from_hbm, loads[0][0]))

    straight, deltas = lax.optimization_barrier((straight, deltas))
    crossed = moved(straight, "ctx", lambda i: i ^ 1)
    returned, held = [], [*q_low]
    for load, offsets, arrived in zip(
        loads[1:], ((2, 2), (3, 1), (1, 3)), (straight, mixed, crossed)
    ):
        last = offsets == (1, 3)
        total, parts, *more = pl.pallas_call(
            functools.partial(pair_kernel, offsets, window, heads, load[1], last),
            in_specs=[in_vmem] * 7 + [in_hbm] * len(load[0]),
            out_specs=[in_vmem] * (2 + len(load[0])),
            out_shape=[
                shape((rows, heads * width), bf16) if last else shape((width, heads * rows), f32),
                shape((2 * rows, width), bf16),
                *loaded(load),
            ],
            scratch_shapes=[pltpu.SemaphoreType.DMA((len(load[0]),))] * (len(load[0]) > 0),
            compiler_params=params,
            cost_estimate=cost(10**6),
            name="block_back_%d%d" % offsets,
        )(arrived, query, grad, mix, norms, deltas, total, *map(from_hbm, load[0]))
        held.extend(more)
        even, odd = offsets
        shift = offsets == (1, 3)
        returned.append(
            moved(parts, "ctx", lambda i: i - 2 if shift and i < 2 else i - (odd if i % 2 else even))
        )

    cols = q_weight.shape[0] // tp_size
    query_term = pl.pallas_call(
        query_term_kernel,
        in_specs=[in_vmem] * 2,
        out_specs=in_vmem,
        out_shape=shape((tp_size, rows, cols), f32),
        compiler_params=params,
        cost_estimate=block_cost,
        name="query_term",
    )(total, held[0])
    for item in returned:
        final = item is returned[-1]
        sums = pl.pallas_call(
            add_kernel,
            in_specs=[in_vmem] * (3 if final else 2),
            out_specs=in_vmem,
            out_shape=shape(sums.shape, bf16 if final else f32),
            compiler_params=params,
            cost_estimate=block_cost,
            name="add_returned",
        )(sums, item, *((query_term,) if final else ()))

    operands = (sums, query_term, *held[1:])
    hops = range(2, tp_size, 2)
    sizes = (cols * 5 // 8, cols * 3 // 8) if cols % 1024 == 0 else (cols // 2,) * 2
    starts = (0, sizes[0])
    low, high = 10**6, block_cost.flops

    def swapped_term(places, after):
        pieces = [(hop, True, start, size) for hop, start, size in places]
        part = term(pieces, operands, None, after, bf16, low, params)
        return part, other_core(part)

    swapped, after = [], ()
    for i in range(2):
        part, item = swapped_term([(hop, starts[i], sizes[i]) for hop in hops], after)
        swapped.append(item)
        after = (part,)
    part, swapped_low = swapped_term([(0, 0, cols // 2)], after)
    part, swapped_high = swapped_term([(0, cols // 2, cols // 2)], (part,))
    sent, after = [[], []], (part,)
    for i in range(2):
        for j, hop in enumerate(hops):
            piece = ((hop, False, starts[i], sizes[i]),)
            part = term(piece, operands, (swapped[i], j * sizes[i]), after, bf16, low, params)
            sent[i].append(moved(part, "tp", lambda k: k + hop))
            after = (part,)
    mine = [
        term(((0, False, j * (cols // 2), cols // 2),), operands, (item, 0), tuple(sent[0][:1]), f32, 10 * high, params)
        for j, item in enumerate((swapped_low, swapped_high))
    ]
    out = ()
    for i in range(2):
        out = pl.pallas_call(
            functools.partial(finish_kernel, starts[i], len(hops)),
            in_specs=[in_vmem] * (2 + len(hops)) + [in_hbm] * len(out),
            out_specs=in_hbm,
            out_shape=shape((rows, cols), bf16),
            input_output_aliases={2 + len(hops): 0} if out else {},
            scratch_shapes=[pltpu.VMEM((rows, sizes[i]), bf16), pltpu.SemaphoreType.DMA],
            compiler_params=params,
            cost_estimate=cost(low),
            name="finish",
        )(*mine, *sent[i], *out)
        out = (out,)
    return out[0]


def solution(mesh):
    return jax.shard_map(
        on_device,
        mesh=mesh,
        in_specs=(
            P("ctx", "tp"),
            P("ctx", "tp"),
            P("ctx", "tp"),
            P("ctx", "tp"),
            P("ctx", "tp"),
            P("ctx", "tp"),
            P("ctx", None),
            P(),
            P(None, "tp"),
            P(None, "tp"),
            P(None, "tp"),
        ),
        out_specs=P("ctx", "tp"),
        check_vma=False,
    )
```

```python
import functools
import math

import jax
import jax.numpy as jnp
from jax import lax
from jax.experimental import pallas as pl
from jax.experimental.pallas import tpu as pltpu
from jax.sharding import PartitionSpec as P

keep_level = 103
keep_scale = 1024.0 / 921.0
log2_e = math.log2(math.e)
f32, bf16, i32 = jnp.float32, jnp.bfloat16, jnp.int32
in_vmem = pl.BlockSpec(memory_space=pltpu.VMEM)
in_hbm = pl.BlockSpec(memory_space=pltpu.HBM)
in_smem = pl.BlockSpec(memory_space=pltpu.SMEM)


def from_hbm(array):
    return pltpu.with_memory_space_constraint(array, pltpu.HBM)


def moved(array, axis, place):
    count = lax.axis_size(axis)
    return lax.ppermute(array, axis, [(i, place(i) % count) for i in range(count)])


def other_core(array):
    return moved(array, "tp", lambda i: i ^ 1)


def by_parity(even, odd):
    return jnp.where(lax.rem(lax.axis_index("ctx"), 2) == 1, odd, even)


def dot(left, right, left_dim, right_dim):
    return lax.dot_general(
        left, right, (((left_dim,), (right_dim,)), ((), ())), preferred_element_type=f32
    )


def keep_mask(mixed):
    mixed = mixed ^ lax.shift_right_logical(mixed, i32(15))
    mixed = mixed * i32(739982445)
    mixed = mixed ^ lax.shift_right_logical(mixed, i32(12))
    mixed = mixed * i32(695872825)
    mixed = mixed ^ lax.shift_right_logical(mixed, i32(15))
    return (mixed & i32(1023)) >= i32(keep_level)


def block_grads(offsets, window, heads, key, value, query_ref, grad_ref, mix_ref, norm_ref, delta_ref):
    rows, width = key.shape
    offset = offsets[0] if offsets[0] == offsets[1] else by_parity(*offsets)
    key_index = lax.broadcasted_iota(i32, (rows, rows), 0)
    query_index = lax.broadcasted_iota(i32, (rows, rows), 1)
    key_part = (key_index - offset * rows) * i32(19349663)
    key_t = key.T
    scale = log2_e * width**-0.5
    key_sum = value_sum = None
    query_parts = []
    for head in range(heads):
        cols = pl.ds(head * width, width)
        query, grad = query_ref[:, cols], grad_ref[:, cols]
        log_norm = norm_ref[pl.ds(offset * heads + head, 1), :]
        row_delta = delta_ref[pl.ds(head, 1), :]
        kept = keep_mask(key_part + mix_ref[pl.ds(head, 1), :])
        probs = jnp.exp2(dot(key, query, 1, 1) * scale - log_norm)
        spacing = query_index - key_index
        if 0 in offsets:
            probs = jnp.where(spacing >= 0, probs, f32(0.0))
        if (max(offsets) + 1) * rows > window:
            probs = jnp.where(spacing < window - offset * rows, probs, f32(0.0))
        dropped = jnp.where(kept, probs, f32(0.0)).astype(bf16)
        grad_probs = dot(value, grad, 1, 1)
        grad_scores = (
            probs * (jnp.where(kept, grad_probs, f32(0.0)) - row_delta)
        ).astype(bf16)
        value_add = dot(dropped, grad, 1, 0)
        key_add = dot(grad_scores, query, 1, 0)
        key_sum = key_add if head == 0 else key_sum + key_add
        value_sum = value_add if head == 0 else value_sum + value_add
        query_parts.append(dot(key_t, grad_scores, 1, 0))
    return key_sum, value_sum, query_parts


def load_kernel(
    heads, key_hbm, value_hbm, query_hbm, grad_hbm, output_hbm, norm_hbm, counter_hbm, mask_hbm,
    key_value, query, grad, output, mix_ref, rows_ref, norm_ref, counter_ref, mask_ref, sems,
):
    rows = key_hbm.shape[0]
    copies = [
        pltpu.make_async_copy(source, target, sems.at[i])
        for i, (source, target) in enumerate(
            (
                (key_hbm, key_value.at[pl.ds(0, rows)]),
                (value_hbm, key_value.at[pl.ds(rows, rows)]),
                (counter_hbm, counter_ref),
                (mask_hbm, mask_ref),
                (norm_hbm, norm_ref),
                (query_hbm, query),
                (grad_hbm, grad),
                (output_hbm, output),
            )
        )
    ]
    for copy in copies:
        copy.start()
    for copy in copies:
        copy.wait()
    block_id = lax.axis_index("ctx")
    first_head = lax.axis_index("tp") * heads
    base = counter_ref[1] + block_id * rows
    common = base * i32(19349663) + counter_ref[0]
    query_pos = lax.broadcasted_iota(i32, (1, rows), 1) + base
    for head in range(heads):
        mix_ref[pl.ds(head, 1), :] = query_pos * i32(73856093) + (
            common + (first_head + head) * i32(83492791)
        )
    norms = norm_ref[...] * f32(log2_e)
    for offset in range(mask_ref.shape[1]):
        active = (block_id >= offset) & (mask_ref[0, offset] == 1)
        rows_ref[pl.ds(offset * heads, heads), :] = jnp.where(active, norms, f32(jnp.inf))


def with_copies(loads, results, refs):
    copies = []
    for i in range(loads):
        copies.append(pltpu.make_async_copy(refs[i], refs[loads + results + i], refs[-1].at[i]))
        copies[-1].start()
    return refs[loads : loads + results], copies


def own_kernel(
    window, heads, key_value_ref, query_ref, grad_ref, output_ref, mix_ref, norm_ref, delta_ref,
    total_ref, sums_ref,
):
    rows, width = key_value_ref.shape[0] // 2, key_value_ref.shape[1]
    lane = lax.broadcasted_iota(i32, (rows, 128), 1)
    packed = jnp.zeros((rows, 128), f32)
    for head in range(heads):
        cols = pl.ds(head * width, width)
        delta = jnp.sum(
            grad_ref[:, cols].astype(f32) * output_ref[:, cols].astype(f32), axis=1, keepdims=True
        )
        packed = jnp.where(lane == head, delta * f32(1.0 / keep_scale), packed)
    delta_ref[...] = packed.T[: delta_ref.shape[0]]
    key_sum, value_sum, query_parts = block_grads(
        (0, 0), window, heads, key_value_ref[:rows], key_value_ref[rows:], query_ref, grad_ref, mix_ref,
        norm_ref, delta_ref,
    )
    grad_scale = keep_scale * width**-0.5
    sums_ref[:rows] = key_sum * f32(grad_scale)
    sums_ref[rows:] = value_sum * f32(keep_scale)
    for head, part in enumerate(query_parts):
        total_ref[:, pl.ds(head * rows, rows)] = part


def pair_kernel(
    offsets, window, heads, loads, last, key_value_ref, query_ref, grad_ref, mix_ref, norm_ref, delta_ref,
    before_ref, *refs,
):
    (total_ref, sums_ref), copies = with_copies(loads, 2, refs)
    rows, width = key_value_ref.shape[0] // 2, key_value_ref.shape[1]
    grad_scale = keep_scale * width**-0.5
    key_sum, value_sum, query_parts = block_grads(
        offsets, window, heads, key_value_ref[:rows], key_value_ref[rows:], query_ref, grad_ref,
        mix_ref, norm_ref, delta_ref,
    )
    sums_ref[:rows] = (key_sum * f32(grad_scale)).astype(bf16)
    sums_ref[rows:] = (value_sum * f32(keep_scale)).astype(bf16)
    for head, part in enumerate(query_parts):
        cols = pl.ds(head * rows, rows)
        if last:
            total_ref[:, pl.ds(head * width, width)] = (
                (before_ref[:, cols] + part).T * f32(grad_scale)
            ).astype(bf16)
        else:
            total_ref[:, cols] = before_ref[:, cols] + part
    for copy in copies:
        copy.wait()


def query_term_kernel(query_ref, wq_ref, wk_ref, wv_ref, out_ref, weight_ref):
    width = wk_ref.shape[1]
    weight_ref[:, :width] = wk_ref[...]
    weight_ref[:, width:] = wv_ref[...]
    places, _, cols = out_ref.shape
    query = query_ref[...]
    for place in range(places):
        out_ref[place] = dot(query, wq_ref[pl.ds(place * cols, cols), :], 1, 1)


def term_kernel(pieces, added, sums_ref, term_ref, weight_ref, *refs):
    count, rows, block = term_ref.shape
    me = lax.axis_index("tp")
    out_ref = refs[-1]
    sums = sums_ref[...]
    done = 0
    for hop, flip, start, cols in pieces:
        place = lax.rem((me + 1 - 2 * lax.rem(me, 2) if flip else me) + hop, count)
        at = pl.ds(pl.multiple_of(place * block + start, 128), cols)
        total = term_ref[place, :, pl.ds(start, cols)]
        total = total + dot(sums, weight_ref[at, :], 1, 1)
        if added is not None:
            total = total + refs[0][:, pl.ds(added + done, cols)].astype(f32)
        out_ref[:, pl.ds(done, cols)] = total.astype(out_ref.dtype)
        done += cols


def term(pieces, operands, added, after, dtype, flops, params):
    rows = operands[1].shape[1]
    first, extra = (None, ()) if added is None else (added[1], added[:1])
    return pl.pallas_call(
        functools.partial(term_kernel, pieces, first),
        in_specs=[in_vmem] * (len(operands) + len(extra) + len(after)),
        out_specs=in_vmem,
        out_shape=jax.ShapeDtypeStruct((rows, sum(piece[3] for piece in pieces)), dtype),
        compiler_params=params,
        cost_estimate=cost(flops),
        name="term",
    )(*operands, *extra, *after)


def add_kernel(left_ref, right_ref, *refs):
    out_ref = refs[-1]
    total = (left_ref[...] + right_ref[...].astype(f32)).astype(out_ref.dtype)
    rows = out_ref.shape[0]
    if rows == total.shape[0]:
        out_ref[...] = total
    else:
        out_ref[...] = jnp.concatenate([total[:rows], total[rows:]], axis=1)


def sum_kernel(first, left_ref, right_ref, out_ref):
    at = pl.ds(first, out_ref.shape[1])
    out_ref[...] = (left_ref[:, at] + right_ref[:, at].astype(f32)).astype(bf16)


def finish_kernel(first, hops, low_ref, high_ref, *refs):
    out_hbm, held, sem = refs[-3:]
    half, size = low_ref.shape[1], held.shape[1]
    for start in range(first, first + size, 128):
        ref, at = (low_ref, start) if start < half else (high_ref, start - half)
        total = ref[:, pl.ds(at, 128)]
        for ref in refs[:hops]:
            total = total + ref[:, pl.ds(start - first, 128)].astype(f32)
        held[:, pl.ds(start - first, 128)] = total.astype(bf16)
    copy = pltpu.make_async_copy(held, out_hbm.at[:, pl.ds(first, size)], sem)
    copy.start()
    copy.wait()


def cost(flops):
    return pl.CostEstimate(flops=flops, bytes_accessed=flops // 400, transcendentals=0)


def on_device(
    queries,
    keys,
    values,
    outputs,
    out_grad,
    log_norm,
    block_mask,
    counter_base,
    q_weight,
    k_weight,
    v_weight,
):
    rows, width = keys.shape
    heads = log_norm.shape[1]
    steps = block_mask.shape[1]
    window = 3 * rows + rows // 2
    tp_size = lax.axis_size("tp")
    params = pltpu.CompilerParams(vmem_limit_bytes=16 * 2**20)

    shape = jax.ShapeDtypeStruct
    key_value, query, grad, output, mix, norms = pl.pallas_call(
        functools.partial(load_kernel, heads),
        in_specs=[in_hbm] * 8,
        out_specs=[in_vmem] * 6,
        out_shape=[
            shape((2 * rows, width), bf16),
            *[shape(queries.shape, bf16)] * 3,
            shape((heads, rows), i32),
            shape((steps * heads, rows), f32),
        ],
        scratch_shapes=[
            pltpu.VMEM((heads, rows), f32),
            pltpu.SMEM(counter_base.shape, i32),
            pltpu.SMEM(block_mask.shape, i32),
            pltpu.SemaphoreType.DMA((8,)),
        ],
        compiler_params=params,
        cost_estimate=pl.CostEstimate(flops=0, bytes_accessed=0, transcendentals=0),
        name="load",
    )(*map(from_hbm, (keys, values, queries, out_grad, outputs, log_norm.T, counter_base, block_mask)))
    straight = moved(key_value, "ctx", lambda i: i + 2)
    count = lax.axis_size("ctx")
    pairs = [(i, i + (3 if i % 2 else 1)) for i in range(count)]
    mixed = lax.ppermute(key_value, "ctx", [pair for pair in pairs if pair[1] < count])
    block_cost = cost(20 * heads * rows * rows * width)

    deltas, total, sums = pl.pallas_call(
        functools.partial(own_kernel, window, heads),
        in_specs=[in_vmem] * 6,
        out_specs=[in_vmem] * 3,
        out_shape=[
            shape((heads, rows), f32),
            shape((width, heads * rows), f32),
            shape((2 * rows, width), f32),
        ],
        compiler_params=params,
        cost_estimate=cost(10**6),
        name="own_block",
    )(key_value, query, grad, output, mix, norms)

    straight, deltas = lax.optimization_barrier((straight, deltas))
    crossed = moved(straight, "ctx", lambda i: i ^ 1)
    returned, held = [], []
    for offsets, arrived in (((2, 2), straight), ((3, 1), mixed), ((1, 3), crossed)):
        load = () if held else (k_weight, v_weight)
        last = offsets == (1, 3)
        total, parts, *more = pl.pallas_call(
            functools.partial(pair_kernel, offsets, window, heads, len(load), last),
            in_specs=[in_vmem] * 7 + [in_hbm] * len(load),
            out_specs=[in_vmem] * (2 + len(load)),
            out_shape=[
                shape((rows, heads * width), bf16) if last else shape((width, heads * rows), f32),
                shape((2 * rows, width), bf16),
                *[shape(item.shape, bf16) for item in load],
            ],
            scratch_shapes=[pltpu.SemaphoreType.DMA((len(load),))] * (len(load) > 0),
            compiler_params=params,
            cost_estimate=cost(10**6),
            name="block_back_%d%d" % offsets,
        )(arrived, query, grad, mix, norms, deltas, total, *map(from_hbm, load))
        held.extend(more)
        even, odd = offsets
        shift = offsets == (1, 3)
        returned.append(
            moved(parts, "ctx", lambda i: i - 2 if shift and i < 2 else i - (odd if i % 2 else even))
        )

    cols = q_weight.shape[0] // tp_size
    query_term, weights = pl.pallas_call(
        query_term_kernel,
        in_specs=[in_vmem] * 4,
        out_specs=[in_vmem] * 2,
        out_shape=[
            shape((tp_size, rows, cols), f32),
            shape((q_weight.shape[0], 2 * width), bf16),
        ],
        compiler_params=params,
        cost_estimate=block_cost,
        name="query_term",
    )(total, q_weight, *held)
    for item in returned:
        final = item is returned[-1]
        sums = pl.pallas_call(
            add_kernel,
            in_specs=[in_vmem] * (3 if final else 2),
            out_specs=in_vmem,
            out_shape=shape((rows, 2 * width), bf16) if final else shape(sums.shape, f32),
            compiler_params=params,
            cost_estimate=block_cost,
            name="add_returned",
        )(sums, item, *((query_term,) if final else ()))

    operands = (sums, query_term, weights)
    hops = range(2, tp_size, 2)
    sizes = (cols * 5 // 8, cols * 3 // 8) if cols % 1024 == 0 else (cols // 2,) * 2
    starts = (0, sizes[0])
    low, high = 10**6, block_cost.flops

    def swapped_term(places, after):
        pieces = [(hop, True, start, size) for hop, start, size in places]
        part = term(pieces, operands, None, after, bf16, low, params)
        return part, other_core(part)

    swapped, after = [], ()
    for i in range(2):
        part, item = swapped_term([(hop, starts[i], sizes[i]) for hop in hops], after)
        swapped.append(item)
        after = (part,)
    part, swapped_low = swapped_term([(0, 0, cols // 2)], after)
    part, swapped_high = swapped_term([(0, cols // 2, cols // 2)], (part,))
    pieces = [(hop, False, starts[0], sizes[0]) for hop in hops]
    ahead = term(pieces, operands, None, (part,), f32, low, params)
    sent, after = [[], []], ()
    for j, hop in enumerate(hops):
        part = pl.pallas_call(
            functools.partial(sum_kernel, j * sizes[0]),
            in_specs=[in_vmem] * 2,
            out_specs=in_vmem,
            out_shape=shape((rows, sizes[0]), bf16),
            compiler_params=params,
            cost_estimate=cost(low),
            name="sum",
        )(ahead, swapped[0])
        sent[0].append(moved(part, "tp", lambda k: k + hop))
        after = (part,)
    for j, hop in enumerate(hops):
        piece = ((hop, False, starts[1], sizes[1]),)
        part = term(piece, operands, (swapped[1], j * sizes[1]), after, bf16, low, params)
        sent[1].append(moved(part, "tp", lambda k: k + hop))
        after = (part,)
    mine = [
        term(((0, False, j * (cols // 2), cols // 2),), operands, (item, 0), tuple(sent[0][:1]), f32, 10 * high, params)
        for j, item in enumerate((swapped_low, swapped_high))
    ]
    out = ()
    for i in range(2):
        out = pl.pallas_call(
            functools.partial(finish_kernel, starts[i], len(hops)),
            in_specs=[in_vmem] * (2 + len(hops)) + [in_hbm] * len(out),
            out_specs=in_hbm,
            out_shape=shape((rows, cols), bf16),
            input_output_aliases={2 + len(hops): 0} if out else {},
            scratch_shapes=[pltpu.VMEM((rows, sizes[i]), bf16), pltpu.SemaphoreType.DMA],
            compiler_params=params,
            cost_estimate=cost(low),
            name="finish",
        )(*mine, *sent[i], *out)
        out = (out,)
    return out[0]


def solution(mesh):
    return jax.shard_map(
        on_device,
        mesh=mesh,
        in_specs=(
            P("ctx", "tp"),
            P("ctx", "tp"),
            P("ctx", "tp"),
            P("ctx", "tp"),
            P("ctx", "tp"),
            P("ctx", "tp"),
            P("ctx", None),
            P(),
            P(None, "tp"),
            P(None, "tp"),
            P(None, "tp"),
        ),
        out_specs=P("ctx", "tp"),
        check_vma=False,
    )
```

```python
import functools
import math

import jax
import jax.numpy as jnp
from jax import lax
from jax.experimental import pallas as pl
from jax.experimental.pallas import tpu as pltpu
from jax.sharding import PartitionSpec as P

keep_level = 103
keep_scale = 1024.0 / 921.0
log2_e = math.log2(math.e)
f32, bf16, i32 = jnp.float32, jnp.bfloat16, jnp.int32
in_vmem = pl.BlockSpec(memory_space=pltpu.VMEM)
in_hbm = pl.BlockSpec(memory_space=pltpu.HBM)
in_smem = pl.BlockSpec(memory_space=pltpu.SMEM)


def from_hbm(array):
    return pltpu.with_memory_space_constraint(array, pltpu.HBM)


def moved(array, axis, place):
    count = lax.axis_size(axis)
    return lax.ppermute(array, axis, [(i, place(i) % count) for i in range(count)])


def other_core(array):
    return moved(array, "tp", lambda i: i ^ 1)


def by_parity(even, odd):
    return jnp.where(lax.rem(lax.axis_index("ctx"), 2) == 1, odd, even)


def dot(left, right, left_dim, right_dim):
    return lax.dot_general(
        left, right, (((left_dim,), (right_dim,)), ((), ())), preferred_element_type=f32
    )


def keep_mask(mixed):
    mixed = mixed ^ lax.shift_right_logical(mixed, i32(15))
    mixed = mixed * i32(739982445)
    mixed = mixed ^ lax.shift_right_logical(mixed, i32(12))
    mixed = mixed * i32(695872825)
    mixed = mixed ^ lax.shift_right_logical(mixed, i32(15))
    return (mixed & i32(1023)) >= i32(keep_level)


def block_grads(offsets, window, heads, key, value, query_ref, grad_ref, mix_ref, norm_ref, delta_ref):
    rows, width = key.shape
    offset = offsets[0] if offsets[0] == offsets[1] else by_parity(*offsets)
    key_index = lax.broadcasted_iota(i32, (rows, rows), 0)
    query_index = lax.broadcasted_iota(i32, (rows, rows), 1)
    key_part = (key_index - offset * rows) * i32(19349663)
    key_t = key.T
    scale = log2_e * width**-0.5
    key_sum = value_sum = None
    query_parts = []
    for head in range(heads):
        cols = pl.ds(head * width, width)
        query, grad = query_ref[:, cols], grad_ref[:, cols]
        log_norm = norm_ref[pl.ds(offset * heads + head, 1), :]
        row_delta = delta_ref[pl.ds(head, 1), :]
        kept = keep_mask(key_part + mix_ref[pl.ds(head, 1), :])
        probs = jnp.exp2(dot(key, query, 1, 1) * scale - log_norm)
        spacing = query_index - key_index
        if 0 in offsets:
            probs = jnp.where(spacing >= 0, probs, f32(0.0))
        if (max(offsets) + 1) * rows > window:
            probs = jnp.where(spacing < window - offset * rows, probs, f32(0.0))
        dropped = jnp.where(kept, probs, f32(0.0)).astype(bf16)
        grad_probs = dot(value, grad, 1, 1)
        grad_scores = (
            probs * (jnp.where(kept, grad_probs, f32(0.0)) - row_delta)
        ).astype(bf16)
        value_add = dot(dropped, grad, 1, 0)
        key_add = dot(grad_scores, query, 1, 0)
        key_sum = key_add if head == 0 else key_sum + key_add
        value_sum = value_add if head == 0 else value_sum + value_add
        query_parts.append(dot(key_t, grad_scores, 1, 0))
    return key_sum, value_sum, query_parts


def load_kernel(
    heads, key_hbm, value_hbm, query_hbm, grad_hbm, output_hbm, norm_hbm, counter_hbm, mask_hbm,
    key_value, query, grad, output, mix_ref, rows_ref, norm_ref, counter_ref, mask_ref, sems,
):
    rows = key_hbm.shape[0]
    copies = [
        pltpu.make_async_copy(source, target, sems.at[i])
        for i, (source, target) in enumerate(
            (
                (key_hbm, key_value.at[pl.ds(0, rows)]),
                (value_hbm, key_value.at[pl.ds(rows, rows)]),
                (counter_hbm, counter_ref),
                (mask_hbm, mask_ref),
                (norm_hbm, norm_ref),
                (query_hbm, query),
                (grad_hbm, grad),
                (output_hbm, output),
            )
        )
    ]
    for copy in copies:
        copy.start()
    for copy in copies:
        copy.wait()
    block_id = lax.axis_index("ctx")
    first_head = lax.axis_index("tp") * heads
    base = counter_ref[1] + block_id * rows
    common = base * i32(19349663) + counter_ref[0]
    query_pos = lax.broadcasted_iota(i32, (1, rows), 1) + base
    for head in range(heads):
        mix_ref[pl.ds(head, 1), :] = query_pos * i32(73856093) + (
            common + (first_head + head) * i32(83492791)
        )
    norms = norm_ref[...] * f32(log2_e)
    for offset in range(mask_ref.shape[1]):
        active = (block_id >= offset) & (mask_ref[0, offset] == 1)
        rows_ref[pl.ds(offset * heads, heads), :] = jnp.where(active, norms, f32(jnp.inf))


def with_copies(loads, results, refs):
    copies = []
    for i in range(loads):
        copies.append(pltpu.make_async_copy(refs[i], refs[loads + results + i], refs[-1].at[i]))
        copies[-1].start()
    return refs[loads : loads + results], copies


def own_kernel(
    window, heads, key_value_ref, query_ref, grad_ref, output_ref, mix_ref, norm_ref, delta_ref,
    total_ref, sums_ref,
):
    rows, width = key_value_ref.shape[0] // 2, key_value_ref.shape[1]
    lane = lax.broadcasted_iota(i32, (rows, 128), 1)
    packed = jnp.zeros((rows, 128), f32)
    for head in range(heads):
        cols = pl.ds(head * width, width)
        delta = jnp.sum(
            grad_ref[:, cols].astype(f32) * output_ref[:, cols].astype(f32), axis=1, keepdims=True
        )
        packed = jnp.where(lane == head, delta * f32(1.0 / keep_scale), packed)
    delta_ref[...] = packed.T[: delta_ref.shape[0]]
    key_sum, value_sum, query_parts = block_grads(
        (0, 0), window, heads, key_value_ref[:rows], key_value_ref[rows:], query_ref, grad_ref, mix_ref,
        norm_ref, delta_ref,
    )
    grad_scale = keep_scale * width**-0.5
    sums_ref[:rows] = key_sum * f32(grad_scale)
    sums_ref[rows:] = value_sum * f32(keep_scale)
    for head, part in enumerate(query_parts):
        total_ref[:, pl.ds(head * rows, rows)] = part


def pair_kernel(
    offsets, window, heads, loads, last, key_value_ref, query_ref, grad_ref, mix_ref, norm_ref, delta_ref,
    before_ref, *refs,
):
    (total_ref, sums_ref), copies = with_copies(loads, 2, refs)
    rows, width = key_value_ref.shape[0] // 2, key_value_ref.shape[1]
    grad_scale = keep_scale * width**-0.5
    key_sum, value_sum, query_parts = block_grads(
        offsets, window, heads, key_value_ref[:rows], key_value_ref[rows:], query_ref, grad_ref,
        mix_ref, norm_ref, delta_ref,
    )
    sums_ref[:rows] = (key_sum * f32(grad_scale)).astype(bf16)
    sums_ref[rows:] = (value_sum * f32(keep_scale)).astype(bf16)
    for head, part in enumerate(query_parts):
        cols = pl.ds(head * rows, rows)
        if last:
            total_ref[:, pl.ds(head * width, width)] = (
                (before_ref[:, cols] + part).T * f32(grad_scale)
            ).astype(bf16)
        else:
            total_ref[:, cols] = before_ref[:, cols] + part
    for copy in copies:
        copy.wait()


def query_term_kernel(query_ref, wk_ref, wv_ref, wq_hbm, out_ref, weight_ref, wq_ref, sems):
    width = wk_ref.shape[1]
    places, _, cols = out_ref.shape
    copies = []
    for place in range(places):
        at = pl.ds(place * cols, cols)
        copies.append(pltpu.make_async_copy(wq_hbm.at[at], wq_ref.at[at], sems.at[place]))
        copies[-1].start()
    weight_ref[:, :width] = wk_ref[...]
    weight_ref[:, width:] = wv_ref[...]
    query = query_ref[...]
    for place, copy in enumerate(copies):
        copy.wait()
        out_ref[place] = dot(query, wq_ref[pl.ds(place * cols, cols), :], 1, 1)


def term_kernel(pieces, added, sums_ref, term_ref, weight_ref, *refs):
    count, rows, block = term_ref.shape
    me = lax.axis_index("tp")
    out_ref = refs[-1]
    sums = sums_ref[...]
    done = 0
    for hop, flip, start, cols in pieces:
        place = lax.rem((me + 1 - 2 * lax.rem(me, 2) if flip else me) + hop, count)
        at = pl.ds(pl.multiple_of(place * block + start, 128), cols)
        total = term_ref[place, :, pl.ds(start, cols)]
        total = total + dot(sums, weight_ref[at, :], 1, 1)
        if added is not None:
            total = total + refs[0][:, pl.ds(added + done, cols)].astype(f32)
        out_ref[:, pl.ds(done, cols)] = total.astype(out_ref.dtype)
        done += cols


def term(pieces, operands, added, after, dtype, flops, params):
    rows = operands[1].shape[1]
    first, extra = (None, ()) if added is None else (added[1], added[:1])
    return pl.pallas_call(
        functools.partial(term_kernel, pieces, first),
        in_specs=[in_vmem] * (len(operands) + len(extra) + len(after)),
        out_specs=in_vmem,
        out_shape=jax.ShapeDtypeStruct((rows, sum(piece[3] for piece in pieces)), dtype),
        compiler_params=params,
        cost_estimate=cost(flops),
        name="term",
    )(*operands, *extra, *after)


def add_kernel(left_ref, right_ref, *refs):
    out_ref = refs[-1]
    total = (left_ref[...] + right_ref[...].astype(f32)).astype(out_ref.dtype)
    rows = out_ref.shape[0]
    if rows == total.shape[0]:
        out_ref[...] = total
    else:
        out_ref[...] = jnp.concatenate([total[:rows], total[rows:]], axis=1)


def sum_kernel(first, left_ref, right_ref, out_ref):
    at = pl.ds(first, out_ref.shape[1])
    out_ref[...] = (left_ref[:, at] + right_ref[:, at].astype(f32)).astype(bf16)


def finish_kernel(first, hops, low_ref, high_ref, *refs):
    out_hbm, held, sem = refs[-3:]
    half, size = low_ref.shape[1], held.shape[1]
    for start in range(first, first + size, 128):
        ref, at = (low_ref, start) if start < half else (high_ref, start - half)
        total = ref[:, pl.ds(at, 128)]
        for ref in refs[:hops]:
            total = total + ref[:, pl.ds(start - first, 128)].astype(f32)
        held[:, pl.ds(start - first, 128)] = total.astype(bf16)
    copy = pltpu.make_async_copy(held, out_hbm.at[:, pl.ds(first, size)], sem)
    copy.start()
    copy.wait()


def cost(flops):
    return pl.CostEstimate(flops=flops, bytes_accessed=flops // 400, transcendentals=0)


def on_device(
    queries,
    keys,
    values,
    outputs,
    out_grad,
    log_norm,
    block_mask,
    counter_base,
    q_weight,
    k_weight,
    v_weight,
):
    rows, width = keys.shape
    heads = log_norm.shape[1]
    steps = block_mask.shape[1]
    window = 3 * rows + rows // 2
    tp_size = lax.axis_size("tp")
    params = pltpu.CompilerParams(vmem_limit_bytes=16 * 2**20)

    shape = jax.ShapeDtypeStruct
    key_value, query, grad, output, mix, norms = pl.pallas_call(
        functools.partial(load_kernel, heads),
        in_specs=[in_hbm] * 8,
        out_specs=[in_vmem] * 6,
        out_shape=[
            shape((2 * rows, width), bf16),
            *[shape(queries.shape, bf16)] * 3,
            shape((heads, rows), i32),
            shape((steps * heads, rows), f32),
        ],
        scratch_shapes=[
            pltpu.VMEM((heads, rows), f32),
            pltpu.SMEM(counter_base.shape, i32),
            pltpu.SMEM(block_mask.shape, i32),
            pltpu.SemaphoreType.DMA((8,)),
        ],
        compiler_params=params,
        cost_estimate=pl.CostEstimate(flops=0, bytes_accessed=0, transcendentals=0),
        name="load",
    )(*map(from_hbm, (keys, values, queries, out_grad, outputs, log_norm.T, counter_base, block_mask)))
    straight = moved(key_value, "ctx", lambda i: i + 2)
    count = lax.axis_size("ctx")
    pairs = [(i, i + (3 if i % 2 else 1)) for i in range(count)]
    mixed = lax.ppermute(key_value, "ctx", [pair for pair in pairs if pair[1] < count])
    block_cost = cost(20 * heads * rows * rows * width)

    deltas, total, sums = pl.pallas_call(
        functools.partial(own_kernel, window, heads),
        in_specs=[in_vmem] * 6,
        out_specs=[in_vmem] * 3,
        out_shape=[
            shape((heads, rows), f32),
            shape((width, heads * rows), f32),
            shape((2 * rows, width), f32),
        ],
        compiler_params=params,
        cost_estimate=cost(10**6),
        name="own_block",
    )(key_value, query, grad, output, mix, norms)

    straight, deltas = lax.optimization_barrier((straight, deltas))
    crossed = moved(straight, "ctx", lambda i: i ^ 1)
    returned, held = [], []
    for offsets, arrived in (((2, 2), straight), ((3, 1), mixed), ((1, 3), crossed)):
        load = () if held else (k_weight, v_weight)
        last = offsets == (1, 3)
        total, parts, *more = pl.pallas_call(
            functools.partial(pair_kernel, offsets, window, heads, len(load), last),
            in_specs=[in_vmem] * 7 + [in_hbm] * len(load),
            out_specs=[in_vmem] * (2 + len(load)),
            out_shape=[
                shape((rows, heads * width), bf16) if last else shape((width, heads * rows), f32),
                shape((2 * rows, width), bf16),
                *[shape(item.shape, bf16) for item in load],
            ],
            scratch_shapes=[pltpu.SemaphoreType.DMA((len(load),))] * (len(load) > 0),
            compiler_params=params,
            cost_estimate=cost(10**6),
            name="block_back_%d%d" % offsets,
        )(arrived, query, grad, mix, norms, deltas, total, *map(from_hbm, load))
        held.extend(more)
        even, odd = offsets
        shift = offsets == (1, 3)
        returned.append(
            moved(parts, "ctx", lambda i: i - 2 if shift and i < 2 else i - (odd if i % 2 else even))
        )

    cols = q_weight.shape[0] // tp_size
    query_term, weights = pl.pallas_call(
        query_term_kernel,
        in_specs=[in_vmem] * 3 + [in_hbm],
        out_specs=[in_vmem] * 2,
        out_shape=[
            shape((tp_size, rows, cols), f32),
            shape((q_weight.shape[0], 2 * width), bf16),
        ],
        scratch_shapes=[
            pltpu.VMEM(q_weight.shape, bf16),
            pltpu.SemaphoreType.DMA((tp_size,)),
        ],
        compiler_params=params,
        cost_estimate=block_cost,
        name="query_term",
    )(total, *held, from_hbm(q_weight))
    for item in returned:
        final = item is returned[-1]
        sums = pl.pallas_call(
            add_kernel,
            in_specs=[in_vmem] * (3 if final else 2),
            out_specs=in_vmem,
            out_shape=shape((rows, 2 * width), bf16) if final else shape(sums.shape, f32),
            compiler_params=params,
            cost_estimate=block_cost,
            name="add_returned",
        )(sums, item, *((query_term,) if final else ()))

    operands = (sums, query_term, weights)
    hops = range(2, tp_size, 2)
    sizes = (cols * 5 // 8, cols * 3 // 8) if cols % 1024 == 0 else (cols // 2,) * 2
    starts = (0, sizes[0])
    low, high = 10**6, block_cost.flops

    def swapped_term(places, after):
        pieces = [(hop, True, start, size) for hop, start, size in places]
        part = term(pieces, operands, None, after, bf16, low, params)
        return part, other_core(part)

    swapped, after = [], ()
    for i in range(2):
        part, item = swapped_term([(hop, starts[i], sizes[i]) for hop in hops], after)
        swapped.append(item)
        after = (part,)
    part, swapped_low = swapped_term([(0, 0, cols // 2)], after)
    part, swapped_high = swapped_term([(0, cols // 2, cols // 2)], (part,))
    pieces = [(hop, False, starts[0], sizes[0]) for hop in hops]
    ahead = term(pieces, operands, None, (part,), f32, low, params)
    sent, after = [[], []], ()
    for j, hop in enumerate(hops):
        part = pl.pallas_call(
            functools.partial(sum_kernel, j * sizes[0]),
            in_specs=[in_vmem] * 2,
            out_specs=in_vmem,
            out_shape=shape((rows, sizes[0]), bf16),
            compiler_params=params,
            cost_estimate=cost(low),
            name="sum",
        )(ahead, swapped[0])
        sent[0].append(moved(part, "tp", lambda k: k + hop))
        after = (part,)
    for j, hop in enumerate(hops):
        piece = ((hop, False, starts[1], sizes[1]),)
        part = term(piece, operands, (swapped[1], j * sizes[1]), after, bf16, low, params)
        sent[1].append(moved(part, "tp", lambda k: k + hop))
        after = (part,)
    mine = [
        term(((0, False, j * (cols // 2), cols // 2),), operands, (item, 0), tuple(sent[0][:1]), f32, 10 * high, params)
        for j, item in enumerate((swapped_low, swapped_high))
    ]
    out = ()
    for i in range(2):
        out = pl.pallas_call(
            functools.partial(finish_kernel, starts[i], len(hops)),
            in_specs=[in_vmem] * (2 + len(hops)) + [in_hbm] * len(out),
            out_specs=in_hbm,
            out_shape=shape((rows, cols), bf16),
            input_output_aliases={2 + len(hops): 0} if out else {},
            scratch_shapes=[pltpu.VMEM((rows, sizes[i]), bf16), pltpu.SemaphoreType.DMA],
            compiler_params=params,
            cost_estimate=cost(low),
            name="finish",
        )(*mine, *sent[i], *out)
        out = (out,)
    return out[0]


def solution(mesh):
    return jax.shard_map(
        on_device,
        mesh=mesh,
        in_specs=(
            P("ctx", "tp"),
            P("ctx", "tp"),
            P("ctx", "tp"),
            P("ctx", "tp"),
            P("ctx", "tp"),
            P("ctx", "tp"),
            P("ctx", None),
            P(),
            P(None, "tp"),
            P(None, "tp"),
            P(None, "tp"),
        ),
        out_specs=P("ctx", "tp"),
        check_vma=False,
    )
```

```python
import functools
import math

import jax
import jax.numpy as jnp
from jax import lax
from jax.experimental import pallas as pl
from jax.experimental.pallas import tpu as pltpu
from jax.sharding import PartitionSpec as P

keep_level = 103
keep_scale = 1024.0 / 921.0
log2_e = math.log2(math.e)
f32, bf16, i32 = jnp.float32, jnp.bfloat16, jnp.int32
in_vmem = pl.BlockSpec(memory_space=pltpu.VMEM)
in_hbm = pl.BlockSpec(memory_space=pltpu.HBM)
in_smem = pl.BlockSpec(memory_space=pltpu.SMEM)


def from_hbm(array):
    return pltpu.with_memory_space_constraint(array, pltpu.HBM)


def moved(array, axis, place):
    count = lax.axis_size(axis)
    return lax.ppermute(array, axis, [(i, place(i) % count) for i in range(count)])


def other_core(array):
    return moved(array, "tp", lambda i: i ^ 1)


def by_parity(even, odd):
    return jnp.where(lax.rem(lax.axis_index("ctx"), 2) == 1, odd, even)


def dot(left, right, left_dim, right_dim):
    return lax.dot_general(
        left, right, (((left_dim,), (right_dim,)), ((), ())), preferred_element_type=f32
    )


def keep_mask(mixed):
    mixed = mixed ^ lax.shift_right_logical(mixed, i32(15))
    mixed = mixed * i32(739982445)
    mixed = mixed ^ lax.shift_right_logical(mixed, i32(12))
    mixed = mixed * i32(695872825)
    mixed = mixed ^ lax.shift_right_logical(mixed, i32(15))
    return (mixed & i32(1023)) >= i32(keep_level)


def block_grads(offsets, window, heads, key, value, query_ref, grad_ref, mix_ref, norm_ref, delta_ref):
    rows, width = key.shape
    offset = offsets[0] if offsets[0] == offsets[1] else by_parity(*offsets)
    key_index = lax.broadcasted_iota(i32, (rows, rows), 0)
    query_index = lax.broadcasted_iota(i32, (rows, rows), 1)
    key_part = (key_index - offset * rows) * i32(19349663)
    key_t = key.T
    scale = log2_e * width**-0.5
    key_sum = value_sum = None
    query_parts = []
    for head in range(heads):
        cols = pl.ds(head * width, width)
        query, grad = query_ref[:, cols], grad_ref[:, cols]
        log_norm = norm_ref[pl.ds(offset * heads + head, 1), :]
        row_delta = delta_ref[pl.ds(head, 1), :]
        kept = keep_mask(key_part + mix_ref[pl.ds(head, 1), :])
        probs = jnp.exp2(dot(key, query, 1, 1) * scale - log_norm)
        spacing = query_index - key_index
        if 0 in offsets:
            probs = jnp.where(spacing >= 0, probs, f32(0.0))
        if (max(offsets) + 1) * rows > window:
            probs = jnp.where(spacing < window - offset * rows, probs, f32(0.0))
        dropped = jnp.where(kept, probs, f32(0.0)).astype(bf16)
        grad_probs = dot(value, grad, 1, 1)
        grad_scores = (
            probs * (jnp.where(kept, grad_probs, f32(0.0)) - row_delta)
        ).astype(bf16)
        value_add = dot(dropped, grad, 1, 0)
        key_add = dot(grad_scores, query, 1, 0)
        key_sum = key_add if head == 0 else key_sum + key_add
        value_sum = value_add if head == 0 else value_sum + value_add
        query_parts.append(dot(key_t, grad_scores, 1, 0))
    return key_sum, value_sum, query_parts


def load_kernel(
    heads, key_hbm, value_hbm, query_hbm, grad_hbm, output_hbm, norm_hbm, counter_hbm, mask_hbm,
    key_value, query, grad, output, mix_ref, rows_ref, norm_ref, counter_ref, mask_ref, sems,
):
    rows = key_hbm.shape[0]
    copies = [
        pltpu.make_async_copy(source, target, sems.at[i])
        for i, (source, target) in enumerate(
            (
                (key_hbm, key_value.at[pl.ds(0, rows)]),
                (value_hbm, key_value.at[pl.ds(rows, rows)]),
                (counter_hbm, counter_ref),
                (mask_hbm, mask_ref),
                (norm_hbm, norm_ref),
                (query_hbm, query),
                (grad_hbm, grad),
                (output_hbm, output),
            )
        )
    ]
    for copy in copies:
        copy.start()
    for copy in copies[2:5]:
        copy.wait()
    block_id = lax.axis_index("ctx")
    first_head = lax.axis_index("tp") * heads
    base = counter_ref[1] + block_id * rows
    common = base * i32(19349663) + counter_ref[0]
    query_pos = lax.broadcasted_iota(i32, (1, rows), 1) + base
    for head in range(heads):
        mix_ref[pl.ds(head, 1), :] = query_pos * i32(73856093) + (
            common + (first_head + head) * i32(83492791)
        )
    norms = norm_ref[...] * f32(log2_e)
    for offset in range(mask_ref.shape[1]):
        active = (block_id >= offset) & (mask_ref[0, offset] == 1)
        rows_ref[pl.ds(offset * heads, heads), :] = jnp.where(active, norms, f32(jnp.inf))
    for copy in copies[:2] + copies[5:]:
        copy.wait()


def with_copies(loads, results, refs):
    copies = []
    for i in range(loads):
        copies.append(pltpu.make_async_copy(refs[i], refs[loads + results + i], refs[-1].at[i]))
        copies[-1].start()
    return refs[loads : loads + results], copies


def own_kernel(
    window, heads, key_value_ref, query_ref, grad_ref, output_ref, mix_ref, norm_ref, delta_ref,
    total_ref, sums_ref,
):
    rows, width = key_value_ref.shape[0] // 2, key_value_ref.shape[1]
    lane = lax.broadcasted_iota(i32, (rows, 128), 1)
    packed = jnp.zeros((rows, 128), f32)
    for head in range(heads):
        cols = pl.ds(head * width, width)
        delta = jnp.sum(
            grad_ref[:, cols].astype(f32) * output_ref[:, cols].astype(f32), axis=1, keepdims=True
        )
        packed = jnp.where(lane == head, delta * f32(1.0 / keep_scale), packed)
    delta_ref[...] = packed.T[: delta_ref.shape[0]]
    key_sum, value_sum, query_parts = block_grads(
        (0, 0), window, heads, key_value_ref[:rows], key_value_ref[rows:], query_ref, grad_ref, mix_ref,
        norm_ref, delta_ref,
    )
    grad_scale = keep_scale * width**-0.5
    sums_ref[:rows] = key_sum * f32(grad_scale)
    sums_ref[rows:] = value_sum * f32(keep_scale)
    for head, part in enumerate(query_parts):
        total_ref[:, pl.ds(head * rows, rows)] = part


def pair_kernel(
    offsets, window, heads, loads, last, key_value_ref, query_ref, grad_ref, mix_ref, norm_ref, delta_ref,
    before_ref, *refs,
):
    (total_ref, sums_ref), copies = with_copies(loads, 2, refs)
    rows, width = key_value_ref.shape[0] // 2, key_value_ref.shape[1]
    grad_scale = keep_scale * width**-0.5
    key_sum, value_sum, query_parts = block_grads(
        offsets, window, heads, key_value_ref[:rows], key_value_ref[rows:], query_ref, grad_ref,
        mix_ref, norm_ref, delta_ref,
    )
    sums_ref[:rows] = (key_sum * f32(grad_scale)).astype(bf16)
    sums_ref[rows:] = (value_sum * f32(keep_scale)).astype(bf16)
    for head, part in enumerate(query_parts):
        cols = pl.ds(head * rows, rows)
        if last:
            total_ref[:, pl.ds(head * width, width)] = (
                (before_ref[:, cols] + part).T * f32(grad_scale)
            ).astype(bf16)
        else:
            total_ref[:, cols] = before_ref[:, cols] + part
    for copy in copies:
        copy.wait()


def query_term_kernel(query_ref, wk_ref, wv_ref, wq_hbm, out_ref, weight_ref, wq_ref, sems):
    width = wk_ref.shape[1]
    places, _, cols = out_ref.shape
    copies = []
    for place in range(places):
        at = pl.ds(place * cols, cols)
        copies.append(pltpu.make_async_copy(wq_hbm.at[at], wq_ref.at[at], sems.at[place]))
        copies[-1].start()
    weight_ref[:, :width] = wk_ref[...]
    weight_ref[:, width:] = wv_ref[...]
    query = query_ref[...]
    for place, copy in enumerate(copies):
        copy.wait()
        out_ref[place] = dot(query, wq_ref[pl.ds(place * cols, cols), :], 1, 1)


def term_kernel(pieces, added, sums_ref, term_ref, weight_ref, *refs):
    count, rows, block = term_ref.shape
    me = lax.axis_index("tp")
    out_ref = refs[-1]
    sums = sums_ref[...]
    done = 0
    for hop, flip, start, cols in pieces:
        place = lax.rem((me + 1 - 2 * lax.rem(me, 2) if flip else me) + hop, count)
        at = pl.ds(pl.multiple_of(place * block + start, 128), cols)
        total = term_ref[place, :, pl.ds(start, cols)]
        total = total + dot(sums, weight_ref[at, :], 1, 1)
        if added is not None:
            total = total + refs[0][:, pl.ds(added + done, cols)].astype(f32)
        out_ref[:, pl.ds(done, cols)] = total.astype(out_ref.dtype)
        done += cols


def term(pieces, operands, added, after, dtype, flops, params):
    rows = operands[1].shape[1]
    first, extra = (None, ()) if added is None else (added[1], added[:1])
    return pl.pallas_call(
        functools.partial(term_kernel, pieces, first),
        in_specs=[in_vmem] * (len(operands) + len(extra) + len(after)),
        out_specs=in_vmem,
        out_shape=jax.ShapeDtypeStruct((rows, sum(piece[3] for piece in pieces)), dtype),
        compiler_params=params,
        cost_estimate=cost(flops),
        name="term",
    )(*operands, *extra, *after)


def add_kernel(left_ref, right_ref, *refs):
    out_ref = refs[-1]
    total = (left_ref[...] + right_ref[...].astype(f32)).astype(out_ref.dtype)
    rows = out_ref.shape[0]
    if rows == total.shape[0]:
        out_ref[...] = total
    else:
        out_ref[...] = jnp.concatenate([total[:rows], total[rows:]], axis=1)


def sum_kernel(first, left_ref, right_ref, out_ref):
    at = pl.ds(first, out_ref.shape[1])
    out_ref[...] = (left_ref[:, at] + right_ref[:, at].astype(f32)).astype(bf16)


def finish_kernel(first, hops, low_ref, high_ref, *refs):
    out_hbm, held, sem = refs[-3:]
    half, size = low_ref.shape[1], held.shape[1]
    for start in range(first, first + size, 128):
        ref, at = (low_ref, start) if start < half else (high_ref, start - half)
        total = ref[:, pl.ds(at, 128)]
        for ref in refs[:hops]:
            total = total + ref[:, pl.ds(start - first, 128)].astype(f32)
        held[:, pl.ds(start - first, 128)] = total.astype(bf16)
    copy = pltpu.make_async_copy(held, out_hbm.at[:, pl.ds(first, size)], sem)
    copy.start()
    copy.wait()


def cost(flops):
    return pl.CostEstimate(flops=flops, bytes_accessed=flops // 400, transcendentals=0)


def on_device(
    queries,
    keys,
    values,
    outputs,
    out_grad,
    log_norm,
    block_mask,
    counter_base,
    q_weight,
    k_weight,
    v_weight,
):
    rows, width = keys.shape
    heads = log_norm.shape[1]
    steps = block_mask.shape[1]
    window = 3 * rows + rows // 2
    tp_size = lax.axis_size("tp")
    params = pltpu.CompilerParams(vmem_limit_bytes=16 * 2**20)

    shape = jax.ShapeDtypeStruct
    key_value, query, grad, output, mix, norms = pl.pallas_call(
        functools.partial(load_kernel, heads),
        in_specs=[in_hbm] * 8,
        out_specs=[in_vmem] * 6,
        out_shape=[
            shape((2 * rows, width), bf16),
            *[shape(queries.shape, bf16)] * 3,
            shape((heads, rows), i32),
            shape((steps * heads, rows), f32),
        ],
        scratch_shapes=[
            pltpu.VMEM((heads, rows), f32),
            pltpu.SMEM(counter_base.shape, i32),
            pltpu.SMEM(block_mask.shape, i32),
            pltpu.SemaphoreType.DMA((8,)),
        ],
        compiler_params=params,
        cost_estimate=pl.CostEstimate(flops=0, bytes_accessed=0, transcendentals=0),
        name="load",
    )(*map(from_hbm, (keys, values, queries, out_grad, outputs, log_norm.T, counter_base, block_mask)))
    straight = moved(key_value, "ctx", lambda i: i + 2)
    count = lax.axis_size("ctx")
    pairs = [(i, i + (3 if i % 2 else 1)) for i in range(count)]
    mixed = lax.ppermute(key_value, "ctx", [pair for pair in pairs if pair[1] < count])
    block_cost = cost(20 * heads * rows * rows * width)

    deltas, total, sums = pl.pallas_call(
        functools.partial(own_kernel, window, heads),
        in_specs=[in_vmem] * 6,
        out_specs=[in_vmem] * 3,
        out_shape=[
            shape((heads, rows), f32),
            shape((width, heads * rows), f32),
            shape((2 * rows, width), f32),
        ],
        compiler_params=params,
        cost_estimate=cost(10**6),
        name="own_block",
    )(key_value, query, grad, output, mix, norms)

    straight, deltas = lax.optimization_barrier((straight, deltas))
    crossed = moved(straight, "ctx", lambda i: i ^ 1)
    returned, held = [], []
    for offsets, arrived in (((2, 2), straight), ((3, 1), mixed), ((1, 3), crossed)):
        load = () if held else (k_weight, v_weight)
        last = offsets == (1, 3)
        total, parts, *more = pl.pallas_call(
            functools.partial(pair_kernel, offsets, window, heads, len(load), last),
            in_specs=[in_vmem] * 7 + [in_hbm] * len(load),
            out_specs=[in_vmem] * (2 + len(load)),
            out_shape=[
                shape((rows, heads * width), bf16) if last else shape((width, heads * rows), f32),
                shape((2 * rows, width), bf16),
                *[shape(item.shape, bf16) for item in load],
            ],
            scratch_shapes=[pltpu.SemaphoreType.DMA((len(load),))] * (len(load) > 0),
            compiler_params=params,
            cost_estimate=cost(10**6),
            name="block_back_%d%d" % offsets,
        )(arrived, query, grad, mix, norms, deltas, total, *map(from_hbm, load))
        held.extend(more)
        even, odd = offsets
        shift = offsets == (1, 3)
        returned.append(
            moved(parts, "ctx", lambda i: i - 2 if shift and i < 2 else i - (odd if i % 2 else even))
        )

    cols = q_weight.shape[0] // tp_size
    query_term, weights = pl.pallas_call(
        query_term_kernel,
        in_specs=[in_vmem] * 3 + [in_hbm],
        out_specs=[in_vmem] * 2,
        out_shape=[
            shape((tp_size, rows, cols), f32),
            shape((q_weight.shape[0], 2 * width), bf16),
        ],
        scratch_shapes=[
            pltpu.VMEM(q_weight.shape, bf16),
            pltpu.SemaphoreType.DMA((tp_size,)),
        ],
        compiler_params=params,
        cost_estimate=block_cost,
        name="query_term",
    )(total, *held, from_hbm(q_weight))
    for item in returned:
        final = item is returned[-1]
        sums = pl.pallas_call(
            add_kernel,
            in_specs=[in_vmem] * (3 if final else 2),
            out_specs=in_vmem,
            out_shape=shape((rows, 2 * width), bf16) if final else shape(sums.shape, f32),
            compiler_params=params,
            cost_estimate=block_cost,
            name="add_returned",
        )(sums, item, *((query_term,) if final else ()))

    operands = (sums, query_term, weights)
    hops = range(2, tp_size, 2)
    sizes = (cols * 3 // 4, cols // 4) if cols % 1024 == 0 else (cols // 2,) * 2
    starts = (0, sizes[0])
    low, high = 10**6, block_cost.flops

    def swapped_term(places, after):
        pieces = [(hop, True, start, size) for hop, start, size in places]
        part = term(pieces, operands, None, after, bf16, low, params)
        return part, other_core(part)

    swapped, after = [], ()
    for i in range(2):
        part, item = swapped_term([(hop, starts[i], sizes[i]) for hop in hops], after)
        swapped.append(item)
        after = (part,)
    part, swapped_low = swapped_term([(0, 0, cols // 2)], after)
    part, swapped_high = swapped_term([(0, cols // 2, cols // 2)], (part,))
    pieces = [(hop, False, starts[0], sizes[0]) for hop in hops]
    ahead = term(pieces, operands, None, (part,), f32, low, params)
    sent, after = [[], []], ()
    for j, hop in enumerate(hops):
        part = pl.pallas_call(
            functools.partial(sum_kernel, j * sizes[0]),
            in_specs=[in_vmem] * 2,
            out_specs=in_vmem,
            out_shape=shape((rows, sizes[0]), bf16),
            compiler_params=params,
            cost_estimate=cost(low),
            name="sum",
        )(ahead, swapped[0])
        sent[0].append(moved(part, "tp", lambda k: k + hop))
        after = (part,)
    for j, hop in enumerate(hops):
        piece = ((hop, False, starts[1], sizes[1]),)
        part = term(piece, operands, (swapped[1], j * sizes[1]), after, bf16, low, params)
        sent[1].append(moved(part, "tp", lambda k: k + hop))
        after = (part,)
    mine = [
        term(((0, False, j * (cols // 2), cols // 2),), operands, (item, 0), tuple(sent[0][:1]), f32, 10 * high, params)
        for j, item in enumerate((swapped_low, swapped_high))
    ]
    out = ()
    for i in range(2):
        out = pl.pallas_call(
            functools.partial(finish_kernel, starts[i], len(hops)),
            in_specs=[in_vmem] * (2 + len(hops)) + [in_hbm] * len(out),
            out_specs=in_hbm,
            out_shape=shape((rows, cols), bf16),
            input_output_aliases={2 + len(hops): 0} if out else {},
            scratch_shapes=[pltpu.VMEM((rows, sizes[i]), bf16), pltpu.SemaphoreType.DMA],
            compiler_params=params,
            cost_estimate=cost(low),
            name="finish",
        )(*mine, *sent[i], *out)
        out = (out,)
    return out[0]


def solution(mesh):
    return jax.shard_map(
        on_device,
        mesh=mesh,
        in_specs=(
            P("ctx", "tp"),
            P("ctx", "tp"),
            P("ctx", "tp"),
            P("ctx", "tp"),
            P("ctx", "tp"),
            P("ctx", "tp"),
            P("ctx", None),
            P(),
            P(None, "tp"),
            P(None, "tp"),
            P(None, "tp"),
        ),
        out_specs=P("ctx", "tp"),
        check_vma=False,
    )
```

```python
import functools
import math

import jax
import jax.numpy as jnp
from jax import lax
from jax.experimental import pallas as pl
from jax.experimental.pallas import tpu as pltpu
from jax.sharding import PartitionSpec as P

keep_level = 103
keep_scale = 1024.0 / 921.0
log2_e = math.log2(math.e)
f32, bf16, i32 = jnp.float32, jnp.bfloat16, jnp.int32
in_vmem = pl.BlockSpec(memory_space=pltpu.VMEM)
in_hbm = pl.BlockSpec(memory_space=pltpu.HBM)
in_smem = pl.BlockSpec(memory_space=pltpu.SMEM)


def from_hbm(array):
    return pltpu.with_memory_space_constraint(array, pltpu.HBM)


def moved(array, axis, place):
    count = lax.axis_size(axis)
    return lax.ppermute(array, axis, [(i, place(i) % count) for i in range(count)])


def other_core(array):
    return moved(array, "tp", lambda i: i ^ 1)


def by_parity(even, odd):
    return jnp.where(lax.rem(lax.axis_index("ctx"), 2) == 1, odd, even)


def dot(left, right, left_dim, right_dim):
    return lax.dot_general(
        left, right, (((left_dim,), (right_dim,)), ((), ())), preferred_element_type=f32
    )


def keep_mask(mixed):
    mixed = mixed ^ lax.shift_right_logical(mixed, i32(15))
    mixed = mixed * i32(739982445)
    mixed = mixed ^ lax.shift_right_logical(mixed, i32(12))
    mixed = mixed * i32(695872825)
    mixed = mixed ^ lax.shift_right_logical(mixed, i32(15))
    return (mixed & i32(1023)) >= i32(keep_level)


def block_grads(offsets, window, heads, key, value, query_ref, grad_ref, mix_ref, norm_ref, delta_ref):
    rows, width = key.shape
    offset = offsets[0] if offsets[0] == offsets[1] else by_parity(*offsets)
    key_index = lax.broadcasted_iota(i32, (rows, rows), 0)
    query_index = lax.broadcasted_iota(i32, (rows, rows), 1)
    key_part = (key_index - offset * rows) * i32(19349663)
    key_t = key.T
    scale = log2_e * width**-0.5
    key_sum = value_sum = None
    query_parts = []
    for head in range(heads):
        cols = pl.ds(head * width, width)
        query, grad = query_ref[:, cols], grad_ref[:, cols]
        log_norm = norm_ref[pl.ds(offset * heads + head, 1), :]
        row_delta = delta_ref[pl.ds(head, 1), :]
        kept = keep_mask(key_part + mix_ref[pl.ds(head, 1), :])
        probs = jnp.exp2(dot(key, query, 1, 1) * scale - log_norm)
        spacing = query_index - key_index
        if 0 in offsets:
            probs = jnp.where(spacing >= 0, probs, f32(0.0))
        if (max(offsets) + 1) * rows > window:
            probs = jnp.where(spacing < window - offset * rows, probs, f32(0.0))
        dropped = jnp.where(kept, probs, f32(0.0)).astype(bf16)
        grad_probs = dot(value, grad, 1, 1)
        grad_scores = (
            probs * (jnp.where(kept, grad_probs, f32(0.0)) - row_delta)
        ).astype(bf16)
        value_add = dot(dropped, grad, 1, 0)
        key_add = dot(grad_scores, query, 1, 0)
        key_sum = key_add if head == 0 else key_sum + key_add
        value_sum = value_add if head == 0 else value_sum + value_add
        query_parts.append(dot(key_t, grad_scores, 1, 0))
    return key_sum, value_sum, query_parts


def load_kernel(
    heads, key_hbm, value_hbm, query_hbm, grad_hbm, output_hbm, norm_hbm, counter_hbm, mask_hbm,
    key_value, query, grad, output, mix_ref, rows_ref, norm_ref, counter_ref, mask_ref, sems,
):
    rows = key_hbm.shape[0]
    copies = [
        pltpu.make_async_copy(source, target, sems.at[i])
        for i, (source, target) in enumerate(
            (
                (key_hbm, key_value.at[pl.ds(0, rows)]),
                (value_hbm, key_value.at[pl.ds(rows, rows)]),
                (counter_hbm, counter_ref),
                (mask_hbm, mask_ref),
                (norm_hbm, norm_ref),
                (query_hbm, query),
                (grad_hbm, grad),
                (output_hbm, output),
            )
        )
    ]
    for copy in copies:
        copy.start()
    for copy in copies[2:5]:
        copy.wait()
    block_id = lax.axis_index("ctx")
    first_head = lax.axis_index("tp") * heads
    base = counter_ref[1] + block_id * rows
    common = base * i32(19349663) + counter_ref[0]
    query_pos = lax.broadcasted_iota(i32, (1, rows), 1) + base
    for head in range(heads):
        mix_ref[pl.ds(head, 1), :] = query_pos * i32(73856093) + (
            common + (first_head + head) * i32(83492791)
        )
    norms = norm_ref[...] * f32(log2_e)
    for offset in range(mask_ref.shape[1]):
        active = (block_id >= offset) & (mask_ref[0, offset] == 1)
        rows_ref[pl.ds(offset * heads, heads), :] = jnp.where(active, norms, f32(jnp.inf))
    for copy in copies[:2] + copies[5:]:
        copy.wait()


def with_copies(loads, results, refs):
    copies = []
    for i in range(loads):
        copies.append(pltpu.make_async_copy(refs[i], refs[loads + results + i], refs[-1].at[i]))
        copies[-1].start()
    return refs[loads : loads + results], copies


def own_kernel(
    window, heads, key_value_ref, query_ref, grad_ref, output_ref, mix_ref, norm_ref, delta_ref,
    total_ref, sums_ref,
):
    rows, width = key_value_ref.shape[0] // 2, key_value_ref.shape[1]
    lane = lax.broadcasted_iota(i32, (rows, 128), 1)
    packed = jnp.zeros((rows, 128), f32)
    for head in range(heads):
        cols = pl.ds(head * width, width)
        delta = jnp.sum(
            grad_ref[:, cols].astype(f32) * output_ref[:, cols].astype(f32), axis=1, keepdims=True
        )
        packed = jnp.where(lane == head, delta * f32(1.0 / keep_scale), packed)
    delta_ref[...] = packed.T[: delta_ref.shape[0]]
    key_sum, value_sum, query_parts = block_grads(
        (0, 0), window, heads, key_value_ref[:rows], key_value_ref[rows:], query_ref, grad_ref, mix_ref,
        norm_ref, delta_ref,
    )
    grad_scale = keep_scale * width**-0.5
    sums_ref[:rows] = key_sum * f32(grad_scale)
    sums_ref[rows:] = value_sum * f32(keep_scale)
    for head, part in enumerate(query_parts):
        total_ref[:, pl.ds(head * rows, rows)] = part


def pair_kernel(
    offsets, window, heads, loads, last, key_value_ref, query_ref, grad_ref, mix_ref, norm_ref, delta_ref,
    before_ref, *refs,
):
    (total_ref, sums_ref), copies = with_copies(loads, 2, refs)
    rows, width = key_value_ref.shape[0] // 2, key_value_ref.shape[1]
    grad_scale = keep_scale * width**-0.5
    key_sum, value_sum, query_parts = block_grads(
        offsets, window, heads, key_value_ref[:rows], key_value_ref[rows:], query_ref, grad_ref,
        mix_ref, norm_ref, delta_ref,
    )
    sums_ref[:rows] = (key_sum * f32(grad_scale)).astype(bf16)
    sums_ref[rows:] = (value_sum * f32(keep_scale)).astype(bf16)
    for head, part in enumerate(query_parts):
        cols = pl.ds(head * rows, rows)
        if last:
            total_ref[:, pl.ds(head * width, width)] = (
                (before_ref[:, cols] + part).T * f32(grad_scale)
            ).astype(bf16)
        else:
            total_ref[:, cols] = before_ref[:, cols] + part
    for copy in copies:
        copy.wait()


def query_term_kernel(query_ref, wq_ref, wk_ref, wv_ref, out_ref, weight_ref):
    width = wk_ref.shape[1]
    weight_ref[:, :width] = wk_ref[...]
    weight_ref[:, width:] = wv_ref[...]
    places, _, cols = out_ref.shape
    query = query_ref[...]
    for place in range(places):
        out_ref[place] = dot(query, wq_ref[pl.ds(place * cols, cols), :], 1, 1)


def term_kernel(pieces, added, sums_ref, term_ref, weight_ref, *refs):
    count, rows, block = term_ref.shape
    me = lax.axis_index("tp")
    out_ref = refs[-1]
    sums = sums_ref[...]
    done = 0
    for hop, flip, start, cols in pieces:
        place = lax.rem((me + 1 - 2 * lax.rem(me, 2) if flip else me) + hop, count)
        at = pl.ds(pl.multiple_of(place * block + start, 128), cols)
        total = term_ref[place, :, pl.ds(start, cols)]
        total = total + dot(sums, weight_ref[at, :], 1, 1)
        if added is not None:
            total = total + refs[0][:, pl.ds(added + done, cols)].astype(f32)
        out_ref[:, pl.ds(done, cols)] = total.astype(out_ref.dtype)
        done += cols


def term(pieces, operands, added, after, dtype, flops, params):
    rows = operands[1].shape[1]
    first, extra = (None, ()) if added is None else (added[1], added[:1])
    return pl.pallas_call(
        functools.partial(term_kernel, pieces, first),
        in_specs=[in_vmem] * (len(operands) + len(extra) + len(after)),
        out_specs=in_vmem,
        out_shape=jax.ShapeDtypeStruct((rows, sum(piece[3] for piece in pieces)), dtype),
        compiler_params=params,
        cost_estimate=cost(flops),
        name="term",
    )(*operands, *extra, *after)


def add_kernel(left_ref, right_ref, *refs):
    out_ref = refs[-1]
    total = (left_ref[...] + right_ref[...].astype(f32)).astype(out_ref.dtype)
    rows = out_ref.shape[0]
    if rows == total.shape[0]:
        out_ref[...] = total
    else:
        out_ref[...] = jnp.concatenate([total[:rows], total[rows:]], axis=1)


def sum_kernel(first, left_ref, right_ref, out_ref):
    at = pl.ds(first, out_ref.shape[1])
    out_ref[...] = (left_ref[:, at] + right_ref[:, at].astype(f32)).astype(bf16)


def finish_kernel(first, hops, low_ref, high_ref, *refs):
    out_hbm, held, sem = refs[-3:]
    half, size = low_ref.shape[1], held.shape[1]
    for start in range(first, first + size, 128):
        ref, at = (low_ref, start) if start < half else (high_ref, start - half)
        total = ref[:, pl.ds(at, 128)]
        for ref in refs[:hops]:
            total = total + ref[:, pl.ds(start - first, 128)].astype(f32)
        held[:, pl.ds(start - first, 128)] = total.astype(bf16)
    copy = pltpu.make_async_copy(held, out_hbm.at[:, pl.ds(first, size)], sem)
    copy.start()
    copy.wait()


def cost(flops):
    return pl.CostEstimate(flops=flops, bytes_accessed=flops // 400, transcendentals=0)


def on_device(
    queries,
    keys,
    values,
    outputs,
    out_grad,
    log_norm,
    block_mask,
    counter_base,
    q_weight,
    k_weight,
    v_weight,
):
    rows, width = keys.shape
    heads = log_norm.shape[1]
    steps = block_mask.shape[1]
    window = 3 * rows + rows // 2
    tp_size = lax.axis_size("tp")
    params = pltpu.CompilerParams(vmem_limit_bytes=16 * 2**20)

    shape = jax.ShapeDtypeStruct
    key_value, query, grad, output, mix, norms = pl.pallas_call(
        functools.partial(load_kernel, heads),
        in_specs=[in_hbm] * 8,
        out_specs=[in_vmem] * 6,
        out_shape=[
            shape((2 * rows, width), bf16),
            *[shape(queries.shape, bf16)] * 3,
            shape((heads, rows), i32),
            shape((steps * heads, rows), f32),
        ],
        scratch_shapes=[
            pltpu.VMEM((heads, rows), f32),
            pltpu.SMEM(counter_base.shape, i32),
            pltpu.SMEM(block_mask.shape, i32),
            pltpu.SemaphoreType.DMA((8,)),
        ],
        compiler_params=params,
        cost_estimate=pl.CostEstimate(flops=0, bytes_accessed=0, transcendentals=0),
        name="load",
    )(*map(from_hbm, (keys, values, queries, out_grad, outputs, log_norm.T, counter_base, block_mask)))
    straight = moved(key_value, "ctx", lambda i: i + 2)
    count = lax.axis_size("ctx")
    pairs = [(i, i + (3 if i % 2 else 1)) for i in range(count)]
    mixed = lax.ppermute(key_value, "ctx", [pair for pair in pairs if pair[1] < count])
    block_cost = cost(20 * heads * rows * rows * width)

    deltas, total, sums = pl.pallas_call(
        functools.partial(own_kernel, window, heads),
        in_specs=[in_vmem] * 6,
        out_specs=[in_vmem] * 3,
        out_shape=[
            shape((heads, rows), f32),
            shape((width, heads * rows), f32),
            shape((2 * rows, width), f32),
        ],
        compiler_params=params,
        cost_estimate=cost(10**6),
        name="own_block",
    )(key_value, query, grad, output, mix, norms)

    straight, deltas = lax.optimization_barrier((straight, deltas))
    crossed = moved(straight, "ctx", lambda i: i ^ 1)
    returned, held = [], []
    for offsets, arrived in (((2, 2), straight), ((3, 1), mixed), ((1, 3), crossed)):
        load = () if held else (k_weight, v_weight)
        last = offsets == (1, 3)
        total, parts, *more = pl.pallas_call(
            functools.partial(pair_kernel, offsets, window, heads, len(load), last),
            in_specs=[in_vmem] * 7 + [in_hbm] * len(load),
            out_specs=[in_vmem] * (2 + len(load)),
            out_shape=[
                shape((rows, heads * width), bf16) if last else shape((width, heads * rows), f32),
                shape((2 * rows, width), bf16),
                *[shape(item.shape, bf16) for item in load],
            ],
            scratch_shapes=[pltpu.SemaphoreType.DMA((len(load),))] * (len(load) > 0),
            compiler_params=params,
            cost_estimate=cost(10**6),
            name="block_back_%d%d" % offsets,
        )(arrived, query, grad, mix, norms, deltas, total, *map(from_hbm, load))
        held.extend(more)
        even, odd = offsets
        shift = offsets == (1, 3)
        returned.append(
            moved(parts, "ctx", lambda i: i - 2 if shift and i < 2 else i - (odd if i % 2 else even))
        )

    cols = q_weight.shape[0] // tp_size
    query_term, weights = pl.pallas_call(
        query_term_kernel,
        in_specs=[in_vmem] * 4,
        out_specs=[in_vmem] * 2,
        out_shape=[
            shape((tp_size, rows, cols), f32),
            shape((q_weight.shape[0], 2 * width), bf16),
        ],
        compiler_params=params,
        cost_estimate=block_cost,
        name="query_term",
    )(total, q_weight, *held)
    for item in returned:
        final = item is returned[-1]
        sums = pl.pallas_call(
            add_kernel,
            in_specs=[in_vmem] * (3 if final else 2),
            out_specs=in_vmem,
            out_shape=shape((rows, 2 * width), bf16) if final else shape(sums.shape, f32),
            compiler_params=params,
            cost_estimate=block_cost,
            name="add_returned",
        )(sums, item, *((query_term,) if final else ()))

    operands = (sums, query_term, weights)
    hops = range(2, tp_size, 2)
    sizes = (cols * 3 // 4, cols // 4) if cols % 1024 == 0 else (cols // 2,) * 2
    starts = (0, sizes[0])
    low, high = 10**6, block_cost.flops

    def swapped_term(places, after):
        pieces = [(hop, True, start, size) for hop, start, size in places]
        part = term(pieces, operands, None, after, bf16, low, params)
        return part, other_core(part)

    swapped, after = [], ()
    for i in range(2):
        part, item = swapped_term([(hop, starts[i], sizes[i]) for hop in hops], after)
        swapped.append(item)
        after = (part,)
    part, swapped_low = swapped_term([(0, 0, cols // 2)], after)
    part, swapped_high = swapped_term([(0, cols // 2, cols // 2)], (part,))
    pieces = [(hop, False, starts[0], sizes[0]) for hop in hops]
    ahead = term(pieces, operands, None, (part,), f32, low, params)
    sent, after = [[], []], ()
    for j, hop in enumerate(hops):
        part = pl.pallas_call(
            functools.partial(sum_kernel, j * sizes[0]),
            in_specs=[in_vmem] * 2,
            out_specs=in_vmem,
            out_shape=shape((rows, sizes[0]), bf16),
            compiler_params=params,
            cost_estimate=cost(low),
            name="sum",
        )(ahead, swapped[0])
        sent[0].append(moved(part, "tp", lambda k: k + hop))
        after = (part,)
    for j, hop in enumerate(hops):
        piece = ((hop, False, starts[1], sizes[1]),)
        part = term(piece, operands, (swapped[1], j * sizes[1]), after, bf16, low, params)
        sent[1].append(moved(part, "tp", lambda k: k + hop))
        after = (part,)
    mine = [
        term(((0, False, j * (cols // 2), cols // 2),), operands, (item, 0), tuple(sent[0][:1]), f32, 10 * high, params)
        for j, item in enumerate((swapped_low, swapped_high))
    ]
    out = ()
    for i in range(2):
        out = pl.pallas_call(
            functools.partial(finish_kernel, starts[i], len(hops)),
            in_specs=[in_vmem] * (2 + len(hops)) + [in_hbm] * len(out),
            out_specs=in_hbm,
            out_shape=shape((rows, cols), bf16),
            input_output_aliases={2 + len(hops): 0} if out else {},
            scratch_shapes=[pltpu.VMEM((rows, sizes[i]), bf16), pltpu.SemaphoreType.DMA],
            compiler_params=params,
            cost_estimate=cost(low),
            name="finish",
        )(*mine, *sent[i], *out)
        out = (out,)
    return out[0]


def solution(mesh):
    return jax.shard_map(
        on_device,
        mesh=mesh,
        in_specs=(
            P("ctx", "tp"),
            P("ctx", "tp"),
            P("ctx", "tp"),
            P("ctx", "tp"),
            P("ctx", "tp"),
            P("ctx", "tp"),
            P("ctx", None),
            P(),
            P(None, "tp"),
            P(None, "tp"),
            P(None, "tp"),
        ),
        out_specs=P("ctx", "tp"),
        check_vma=False,
    )
```

```python
import functools
import math

import jax
import jax.numpy as jnp
from jax import lax
from jax.experimental import pallas as pl
from jax.experimental.pallas import tpu as pltpu
from jax.sharding import PartitionSpec as P

keep_level = 103
keep_scale = 1024.0 / 921.0
log2_e = math.log2(math.e)
f32, bf16, i32 = jnp.float32, jnp.bfloat16, jnp.int32
in_vmem = pl.BlockSpec(memory_space=pltpu.VMEM)
in_hbm = pl.BlockSpec(memory_space=pltpu.HBM)
in_smem = pl.BlockSpec(memory_space=pltpu.SMEM)


def from_hbm(array):
    return pltpu.with_memory_space_constraint(array, pltpu.HBM)


def moved(array, axis, place):
    count = lax.axis_size(axis)
    return lax.ppermute(array, axis, [(i, place(i) % count) for i in range(count)])


def other_core(array):
    return moved(array, "tp", lambda i: i ^ 1)


def by_parity(even, odd):
    return jnp.where(lax.rem(lax.axis_index("ctx"), 2) == 1, odd, even)


def dot(left, right, left_dim, right_dim):
    return lax.dot_general(
        left, right, (((left_dim,), (right_dim,)), ((), ())), preferred_element_type=f32
    )


def keep_mask(mixed):
    mixed = mixed ^ lax.shift_right_logical(mixed, i32(15))
    mixed = mixed * i32(739982445)
    mixed = mixed ^ lax.shift_right_logical(mixed, i32(12))
    mixed = mixed * i32(695872825)
    mixed = mixed ^ lax.shift_right_logical(mixed, i32(15))
    return (mixed & i32(1023)) >= i32(keep_level)


def block_grads(offsets, window, heads, key, value, query_ref, grad_ref, mix_ref, norm_ref, delta_ref):
    rows, width = key.shape
    offset = offsets[0] if offsets[0] == offsets[1] else by_parity(*offsets)
    key_index = lax.broadcasted_iota(i32, (rows, rows), 0)
    query_index = lax.broadcasted_iota(i32, (rows, rows), 1)
    key_part = (key_index - offset * rows) * i32(19349663)
    key_t = key.T
    scale = log2_e * width**-0.5
    key_sum = value_sum = None
    query_parts = []
    for head in range(heads):
        cols = pl.ds(head * width, width)
        query, grad = query_ref[:, cols], grad_ref[:, cols]
        log_norm = norm_ref[pl.ds(offset * heads + head, 1), :]
        row_delta = delta_ref[pl.ds(head, 1), :]
        kept = keep_mask(key_part + mix_ref[pl.ds(head, 1), :])
        probs = jnp.exp2(dot(key, query, 1, 1) * scale - log_norm)
        spacing = query_index - key_index
        if 0 in offsets:
            probs = jnp.where(spacing >= 0, probs, f32(0.0))
        if (max(offsets) + 1) * rows > window:
            probs = jnp.where(spacing < window - offset * rows, probs, f32(0.0))
        dropped = jnp.where(kept, probs, f32(0.0)).astype(bf16)
        grad_probs = dot(value, grad, 1, 1)
        grad_scores = (
            probs * (jnp.where(kept, grad_probs, f32(0.0)) - row_delta)
        ).astype(bf16)
        value_add = dot(dropped, grad, 1, 0)
        key_add = dot(grad_scores, query, 1, 0)
        key_sum = key_add if head == 0 else key_sum + key_add
        value_sum = value_add if head == 0 else value_sum + value_add
        query_parts.append(dot(key_t, grad_scores, 1, 0))
    return key_sum, value_sum, query_parts


def load_kernel(
    heads, key_hbm, value_hbm, query_hbm, grad_hbm, output_hbm, norm_hbm, counter_hbm, mask_hbm,
    key_value, query, grad, output, mix_ref, rows_ref, norm_ref, counter_ref, mask_ref, sems,
):
    rows = key_hbm.shape[0]
    copies = [
        pltpu.make_async_copy(source, target, sems.at[i])
        for i, (source, target) in enumerate(
            (
                (key_hbm, key_value.at[pl.ds(0, rows)]),
                (value_hbm, key_value.at[pl.ds(rows, rows)]),
                (counter_hbm, counter_ref),
                (mask_hbm, mask_ref),
                (norm_hbm, norm_ref),
                (query_hbm, query),
                (grad_hbm, grad),
                (output_hbm, output),
            )
        )
    ]
    for copy in copies:
        copy.start()
    for copy in copies:
        copy.wait()
    block_id = lax.axis_index("ctx")
    first_head = lax.axis_index("tp") * heads
    base = counter_ref[1] + block_id * rows
    common = base * i32(19349663) + counter_ref[0]
    query_pos = lax.broadcasted_iota(i32, (1, rows), 1) + base
    for head in range(heads):
        mix_ref[pl.ds(head, 1), :] = query_pos * i32(73856093) + (
            common + (first_head + head) * i32(83492791)
        )
    norms = norm_ref[...] * f32(log2_e)
    for offset in range(mask_ref.shape[1]):
        active = (block_id >= offset) & (mask_ref[0, offset] == 1)
        rows_ref[pl.ds(offset * heads, heads), :] = jnp.where(active, norms, f32(jnp.inf))


def with_copies(loads, results, refs):
    copies = []
    for i in range(loads):
        copies.append(pltpu.make_async_copy(refs[i], refs[loads + results + i], refs[-1].at[i]))
        copies[-1].start()
    return refs[loads : loads + results], copies


def own_kernel(
    window, heads, key_value_ref, query_ref, grad_ref, output_ref, mix_ref, norm_ref, delta_ref,
    total_ref, sums_ref,
):
    rows, width = key_value_ref.shape[0] // 2, key_value_ref.shape[1]
    lane = lax.broadcasted_iota(i32, (rows, 128), 1)
    packed = jnp.zeros((rows, 128), f32)
    for head in range(heads):
        cols = pl.ds(head * width, width)
        delta = jnp.sum(
            grad_ref[:, cols].astype(f32) * output_ref[:, cols].astype(f32), axis=1, keepdims=True
        )
        packed = jnp.where(lane == head, delta * f32(1.0 / keep_scale), packed)
    delta_ref[...] = packed.T[: delta_ref.shape[0]]
    key_sum, value_sum, query_parts = block_grads(
        (0, 0), window, heads, key_value_ref[:rows], key_value_ref[rows:], query_ref, grad_ref, mix_ref,
        norm_ref, delta_ref,
    )
    grad_scale = keep_scale * width**-0.5
    sums_ref[:rows] = key_sum * f32(grad_scale)
    sums_ref[rows:] = value_sum * f32(keep_scale)
    for head, part in enumerate(query_parts):
        total_ref[:, pl.ds(head * rows, rows)] = part


def pair_kernel(
    offsets, window, heads, loads, last, key_value_ref, query_ref, grad_ref, mix_ref, norm_ref, delta_ref,
    before_ref, *refs,
):
    (total_ref, sums_ref), copies = with_copies(loads, 2, refs)
    rows, width = key_value_ref.shape[0] // 2, key_value_ref.shape[1]
    grad_scale = keep_scale * width**-0.5
    key_sum, value_sum, query_parts = block_grads(
        offsets, window, heads, key_value_ref[:rows], key_value_ref[rows:], query_ref, grad_ref,
        mix_ref, norm_ref, delta_ref,
    )
    sums_ref[:rows] = (key_sum * f32(grad_scale)).astype(bf16)
    sums_ref[rows:] = (value_sum * f32(keep_scale)).astype(bf16)
    for head, part in enumerate(query_parts):
        cols = pl.ds(head * rows, rows)
        if last:
            total_ref[:, pl.ds(head * width, width)] = (
                (before_ref[:, cols] + part).T * f32(grad_scale)
            ).astype(bf16)
        else:
            total_ref[:, cols] = before_ref[:, cols] + part
    for copy in copies:
        copy.wait()


def query_term_kernel(query_ref, wq_ref, wk_ref, wv_ref, out_ref, weight_ref):
    width = wk_ref.shape[1]
    weight_ref[:, :width] = wk_ref[...]
    weight_ref[:, width:] = wv_ref[...]
    places, _, cols = out_ref.shape
    query = query_ref[...]
    for place in range(places):
        out_ref[place] = dot(query, wq_ref[pl.ds(place * cols, cols), :], 1, 1)


def term_kernel(pieces, added, sums_ref, term_ref, weight_ref, *refs):
    count, rows, block = term_ref.shape
    me = lax.axis_index("tp")
    out_ref = refs[-1]
    sums = sums_ref[...]
    done = 0
    for hop, flip, start, cols in pieces:
        place = lax.rem((me + 1 - 2 * lax.rem(me, 2) if flip else me) + hop, count)
        at = pl.ds(pl.multiple_of(place * block + start, 128), cols)
        total = term_ref[place, :, pl.ds(start, cols)]
        total = total + dot(sums, weight_ref[at, :], 1, 1)
        if added is not None:
            total = total + refs[0][:, pl.ds(added + done, cols)].astype(f32)
        out_ref[:, pl.ds(done, cols)] = total.astype(out_ref.dtype)
        done += cols


def term(pieces, operands, added, after, dtype, flops, params):
    rows = operands[1].shape[1]
    first, extra = (None, ()) if added is None else (added[1], added[:1])
    return pl.pallas_call(
        functools.partial(term_kernel, pieces, first),
        in_specs=[in_vmem] * (len(operands) + len(extra) + len(after)),
        out_specs=in_vmem,
        out_shape=jax.ShapeDtypeStruct((rows, sum(piece[3] for piece in pieces)), dtype),
        compiler_params=params,
        cost_estimate=cost(flops),
        name="term",
    )(*operands, *extra, *after)


def add_kernel(left_ref, right_ref, *refs):
    out_ref = refs[-1]
    total = (left_ref[...] + right_ref[...].astype(f32)).astype(out_ref.dtype)
    rows = out_ref.shape[0]
    if rows == total.shape[0]:
        out_ref[...] = total
    else:
        out_ref[...] = jnp.concatenate([total[:rows], total[rows:]], axis=1)


def sum_kernel(first, left_ref, right_ref, out_ref):
    at = pl.ds(first, out_ref.shape[1])
    out_ref[...] = (left_ref[:, at] + right_ref[:, at].astype(f32)).astype(bf16)


def finish_kernel(first, hops, low_ref, high_ref, *refs):
    out_hbm, held, sem = refs[-3:]
    half, size = low_ref.shape[1], held.shape[1]
    copies = []
    for start in range(first, first + size, 128):
        ref, at = (low_ref, start) if start < half else (high_ref, start - half)
        total = ref[:, pl.ds(at, 128)]
        for ref in refs[:hops]:
            total = total + ref[:, pl.ds(start - first, 128)].astype(f32)
        held[:, pl.ds(start - first, 128)] = total.astype(bf16)
        copies.append(
            pltpu.make_async_copy(
                held.at[:, pl.ds(start - first, 128)],
                out_hbm.at[:, pl.ds(start, 128)],
                sem.at[len(copies)],
            )
        )
        copies[-1].start()
    for copy in copies:
        copy.wait()


def cost(flops):
    return pl.CostEstimate(flops=flops, bytes_accessed=flops // 400, transcendentals=0)


def on_device(
    queries,
    keys,
    values,
    outputs,
    out_grad,
    log_norm,
    block_mask,
    counter_base,
    q_weight,
    k_weight,
    v_weight,
):
    rows, width = keys.shape
    heads = log_norm.shape[1]
    steps = block_mask.shape[1]
    window = 3 * rows + rows // 2
    tp_size = lax.axis_size("tp")
    params = pltpu.CompilerParams(vmem_limit_bytes=16 * 2**20)

    shape = jax.ShapeDtypeStruct
    key_value, query, grad, output, mix, norms = pl.pallas_call(
        functools.partial(load_kernel, heads),
        in_specs=[in_hbm] * 8,
        out_specs=[in_vmem] * 6,
        out_shape=[
            shape((2 * rows, width), bf16),
            *[shape(queries.shape, bf16)] * 3,
            shape((heads, rows), i32),
            shape((steps * heads, rows), f32),
        ],
        scratch_shapes=[
            pltpu.VMEM((heads, rows), f32),
            pltpu.SMEM(counter_base.shape, i32),
            pltpu.SMEM(block_mask.shape, i32),
            pltpu.SemaphoreType.DMA((8,)),
        ],
        compiler_params=params,
        cost_estimate=pl.CostEstimate(flops=0, bytes_accessed=0, transcendentals=0),
        name="load",
    )(*map(from_hbm, (keys, values, queries, out_grad, outputs, log_norm.T, counter_base, block_mask)))
    straight = moved(key_value, "ctx", lambda i: i + 2)
    count = lax.axis_size("ctx")
    pairs = [(i, i + (3 if i % 2 else 1)) for i in range(count)]
    mixed = lax.ppermute(key_value, "ctx", [pair for pair in pairs if pair[1] < count])
    block_cost = cost(20 * heads * rows * rows * width)

    deltas, total, sums = pl.pallas_call(
        functools.partial(own_kernel, window, heads),
        in_specs=[in_vmem] * 6,
        out_specs=[in_vmem] * 3,
        out_shape=[
            shape((heads, rows), f32),
            shape((width, heads * rows), f32),
            shape((2 * rows, width), f32),
        ],
        compiler_params=params,
        cost_estimate=cost(10**6),
        name="own_block",
    )(key_value, query, grad, output, mix, norms)

    straight, deltas = lax.optimization_barrier((straight, deltas))
    crossed = moved(straight, "ctx", lambda i: i ^ 1)
    returned, held = [], []
    for offsets, arrived in (((2, 2), straight), ((3, 1), mixed), ((1, 3), crossed)):
        load = () if held else (k_weight, v_weight)
        last = offsets == (1, 3)
        total, parts, *more = pl.pallas_call(
            functools.partial(pair_kernel, offsets, window, heads, len(load), last),
            in_specs=[in_vmem] * 7 + [in_hbm] * len(load),
            out_specs=[in_vmem] * (2 + len(load)),
            out_shape=[
                shape((rows, heads * width), bf16) if last else shape((width, heads * rows), f32),
                shape((2 * rows, width), bf16),
                *[shape(item.shape, bf16) for item in load],
            ],
            scratch_shapes=[pltpu.SemaphoreType.DMA((len(load),))] * (len(load) > 0),
            compiler_params=params,
            cost_estimate=cost(10**6),
            name="block_back_%d%d" % offsets,
        )(arrived, query, grad, mix, norms, deltas, total, *map(from_hbm, load))
        held.extend(more)
        even, odd = offsets
        shift = offsets == (1, 3)
        returned.append(
            moved(parts, "ctx", lambda i: i - 2 if shift and i < 2 else i - (odd if i % 2 else even))
        )

    cols = q_weight.shape[0] // tp_size
    query_term, weights = pl.pallas_call(
        query_term_kernel,
        in_specs=[in_vmem] * 4,
        out_specs=[in_vmem] * 2,
        out_shape=[
            shape((tp_size, rows, cols), f32),
            shape((q_weight.shape[0], 2 * width), bf16),
        ],
        compiler_params=params,
        cost_estimate=block_cost,
        name="query_term",
    )(total, q_weight, *held)
    for item in returned:
        final = item is returned[-1]
        sums = pl.pallas_call(
            add_kernel,
            in_specs=[in_vmem] * (3 if final else 2),
            out_specs=in_vmem,
            out_shape=shape((rows, 2 * width), bf16) if final else shape(sums.shape, f32),
            compiler_params=params,
            cost_estimate=block_cost,
            name="add_returned",
        )(sums, item, *((query_term,) if final else ()))

    operands = (sums, query_term, weights)
    hops = range(2, tp_size, 2)
    sizes = (cols * 5 // 8, cols * 3 // 8) if cols % 1024 == 0 else (cols // 2,) * 2
    starts = (0, sizes[0])
    low, high = 10**6, block_cost.flops

    def swapped_term(places, after):
        pieces = [(hop, True, start, size) for hop, start, size in places]
        part = term(pieces, operands, None, after, bf16, low, params)
        return part, other_core(part)

    swapped, after = [], ()
    for i in range(2):
        part, item = swapped_term([(hop, starts[i], sizes[i]) for hop in hops], after)
        swapped.append(item)
        after = (part,)
    part, swapped_low = swapped_term([(0, 0, cols // 2)], after)
    part, swapped_high = swapped_term([(0, cols // 2, cols // 2)], (part,))
    pieces = [(hop, False, starts[0], sizes[0]) for hop in hops]
    ahead = term(pieces, operands, None, (part,), f32, low, params)
    sent, after = [[], []], ()
    for j, hop in enumerate(hops):
        part = pl.pallas_call(
            functools.partial(sum_kernel, j * sizes[0]),
            in_specs=[in_vmem] * 2,
            out_specs=in_vmem,
            out_shape=shape((rows, sizes[0]), bf16),
            compiler_params=params,
            cost_estimate=cost(low),
            name="sum",
        )(ahead, swapped[0])
        sent[0].append(moved(part, "tp", lambda k: k + hop))
        after = (part,)
    for j, hop in enumerate(hops):
        piece = ((hop, False, starts[1], sizes[1]),)
        part = term(piece, operands, (swapped[1], j * sizes[1]), after, bf16, low, params)
        sent[1].append(moved(part, "tp", lambda k: k + hop))
        after = (part,)
    mine = [
        term(((0, False, j * (cols // 2), cols // 2),), operands, (item, 0), tuple(sent[0][:1]), f32, 10 * high, params)
        for j, item in enumerate((swapped_low, swapped_high))
    ]
    out = ()
    for i in range(2):
        out = pl.pallas_call(
            functools.partial(finish_kernel, starts[i], len(hops)),
            in_specs=[in_vmem] * (2 + len(hops)) + [in_hbm] * len(out),
            out_specs=in_hbm,
            out_shape=shape((rows, cols), bf16),
            input_output_aliases={2 + len(hops): 0} if out else {},
            scratch_shapes=[
                pltpu.VMEM((rows, sizes[i]), bf16),
                pltpu.SemaphoreType.DMA((sizes[i] // 128,)),
            ],
            compiler_params=params,
            cost_estimate=cost(low),
            name="finish",
        )(*mine, *sent[i], *out)
        out = (out,)
    return out[0]


def solution(mesh):
    return jax.shard_map(
        on_device,
        mesh=mesh,
        in_specs=(
            P("ctx", "tp"),
            P("ctx", "tp"),
            P("ctx", "tp"),
            P("ctx", "tp"),
            P("ctx", "tp"),
            P("ctx", "tp"),
            P("ctx", None),
            P(),
            P(None, "tp"),
            P(None, "tp"),
            P(None, "tp"),
        ),
        out_specs=P("ctx", "tp"),
        check_vma=False,
    )
```
